256 devices in a mesh: seq: 2 (over core), tp: 8 (over y, x_lo), section: 16 (over z, x_hi).
Axes of the slice: x: 4 (x_hi: 2, x_lo: 2; x = x_hi * 2 + x_lo), y: 4, z: 8, core: 2. Of those that a mesh axis runs over, the one named last changes fastest.
Arguments:
- hidden: bfloat16 [16384, 4096], P(('seq', 'section'), 'tp'), may hold values from -6 to 6
- gain: bfloat16 [4096], replicated, may hold values from 0.5 to 1.5
- trace_emb: bfloat16 [16384, 1024], P(('seq', 'section'), 'tp')
- counts: int32 [256], P(('seq', 'section')), may hold values from 0 to 4, as said below
- offsets: int32 [256, 4], P(('seq', 'section')), may hold values from 2 to 255, as said below
- w_stretch_kv: bfloat16 [4096, 2048], P(None, 'tp'), may hold values from -0.09375 to 0.09375
- encoder_query_weight: bfloat16 [1024, 1024], P('section'), may hold values from -0.1875 to 0.1875
- encoder_output_weight: bfloat16 [1024, 1024], P('section'), may hold values from -0.1875 to 0.1875
- w_cca_q: bfloat16 [4096, 2048], P(None, 'tp'), may hold values from -0.09375 to 0.09375
- w_cca_kv: bfloat16 [1024, 4096], P(None, 'tp'), may hold values from -0.1875 to 0.1875
- w_cca_o: bfloat16 [2048, 4096], P('tp'), may hold values from -0.1875 to 0.1875
Outputs:
- block_out: bfloat16 [16384, 4096], P(('seq', 'section'), 'tp')
The draws below stay inside these ranges and needn't reach their ends.
Inputs may be any that keep to these rules, and one draw needn't show every extreme that they name: counts[u] is 0 for the first two stretches; the last stretch has 4. `offsets`: for stretch u >= 2 each offset lies in 2 to u, so a neighbour ends before its stretch; for u < 2 it is 2.
All inputs are finite; a program needn't handle non-finite values.
Results may differ from the reference program's by a relative error of at most 0.02.
Values may be sent and summed in bfloat16 or wider, within the bound.
A program may use at most 128 MiB of HBM per device.

```python
import math
import jax
import jax.numpy as jnp
from jax import lax

D = 4096
DH = 128
HQ = 16
DE = 1024
STRETCH_TOKENS = 64
KNB = 4
NLEN = 128
TOKENS = 16384
STRETCHES = 256


def draw_trace_emb(key, part):
    key = jax.random.fold_in(key, 11)
    base = jax.random.normal(key, (TOKENS, DE), jnp.float32)
    return base.astype(jnp.bfloat16)


def draw_counts(key, part):
    key = jax.random.fold_in(key, 3)
    drawn = jax.random.randint(key, (STRETCHES,), 0, KNB + 1)
    index = jnp.arange(STRETCHES)
    drawn = jnp.where(index < 2, 0, drawn)
    return drawn.at[STRETCHES - 1].set(KNB).astype(jnp.int32)


def draw_offsets(key, part):
    key = jax.random.fold_in(key, 5)
    drawn = jax.random.randint(key, (STRETCHES, KNB), 0, 1 << 20)
    index = jnp.arange(STRETCHES)[:, None]
    span = jnp.maximum(index - 1, 1)
    result = 2 + drawn % span
    return result.at[STRETCHES - 1, 0].set(STRETCHES - 1).astype(jnp.int32)


def with_spikes(values, own_key, source, target, blocks, factor):
    def block_of(axis_at):
        return (jnp.arange(values.shape[axis_at]) // (values.shape[axis_at] // blocks)).reshape((-1,) + (1,) * (values.ndim - 1 - axis_at))

    near = jax.random.permutation(own_key, blocks)[block_of(target)]
    second = (block_of(target) + blocks // 2) % blocks
    return jnp.where((block_of(source) == near) | (block_of(source) == second), factor * values, values)


def block_scale(key, extent, cuts, least, high):
    level = 1.0
    for position, parts in cuts:
        draws = jax.random.uniform(jax.random.fold_in(jax.random.fold_in(key, 6), position), (parts,), jnp.float32, least / len(cuts), high / len(cuts))
        level = level * jnp.repeat(jnp.exp(draws), extent[position] // parts).reshape((-1,) + (1,) * (len(extent) - 1 - position))
    return level


def gaussian(rng, extent, deviation, most, split=(), kind=jnp.bfloat16):
    level = block_scale(rng, extent, split, -0.22, 0.18) if split else 1.0
    array = jax.random.normal(rng, extent, jnp.float32) * deviation * level
    return jnp.minimum(jnp.maximum(array, -most), most).astype(kind)


def noise_with(own_key, extent, spread, most, cuts, heavy, kind=jnp.bfloat16):
    entries = spread * jax.random.normal(own_key, extent, jnp.float32)
    if cuts:
        entries = entries * block_scale(own_key, extent, cuts, -0.22, 0.18)
    return jnp.clip(with_spikes(entries, jax.random.fold_in(own_key, 3), *heavy), -most, most).astype(kind)


def setup_inputs(seed: int = 0) -> dict:
    keys = jax.random.split(jax.random.key(seed), 12)
    hidden = gaussian(keys[0], (TOKENS, D), 1.0, 6.0, ((0, 32), (1, 8)))
    gain = jnp.clip(1.0 + 0.1 * jax.random.normal(keys[1], (D,), jnp.float32), 0.5, 1.5).astype(jnp.bfloat16)
    trace_emb = draw_trace_emb(jax.random.fold_in(keys[11], 71), 0)
    counts = draw_counts(jax.random.fold_in(keys[11], 71), 0)
    offsets = draw_offsets(jax.random.fold_in(keys[11], 71), 0)
    w_stretch_kv = gaussian(keys[5], (D, 2 * DE), D ** -0.5, 0.09375, ((1, 8),))
    encoder_query_weight = gaussian(keys[6], (DE, DE), DE ** -0.5, 0.1875, ((0, 16),))
    encoder_output_weight = gaussian(keys[7], (DE, DE), DE ** -0.5, 0.1875, ((0, 16),))
    w_cca_q = gaussian(keys[8], (D, HQ * DH), D ** -0.5, 0.09375, ((1, 8),))
    w_cca_kv = gaussian(keys[9], (DE, 2 * HQ * DH), DE ** -0.5, 0.1875, ((1, 8),))
    w_cca_o = noise_with(keys[10], (HQ * DH, D), (HQ * DH) ** -0.5, 0.1875, ((0, 8),), (0, 1, 8, 2.0))
    return dict(hidden=hidden, gain=gain, trace_emb=trace_emb, counts=counts, offsets=offsets, w_stretch_kv=w_stretch_kv, encoder_query_weight=encoder_query_weight, encoder_output_weight=encoder_output_weight, w_cca_q=w_cca_q, w_cca_kv=w_cca_kv, w_cca_o=w_cca_o)


EPS = 1e-05
NEG = -1e+30

def rms_scale(rows, gain):
    wide = rows.astype(jnp.float32)
    inverse = lax.rsqrt(lax.optimization_barrier(jnp.mean(wide * wide, axis=-1, keepdims=True)) + EPS)
    return (wide * inverse * gain.astype(jnp.float32)).astype(jnp.bfloat16)

def encode_neighbours(row_count, stretch_key_values, encoder_query_weight, encoder_output_weight):
    number, keys_n, width = row_count.shape
    heads = encoder_query_weight.shape[1] // DH
    factor = 1.0 / math.sqrt(DH)
    flat = row_count.reshape(number * keys_n, width)
    query = jnp.dot(flat, encoder_query_weight, preferred_element_type=jnp.float32).astype(jnp.bfloat16)
    query = query.reshape(number, keys_n, heads, DH)
    paired = stretch_key_values.reshape(number, stretch_key_values.shape[1], heads, 2, DH)
    scores = jnp.einsum('cnhd,cmhd->chnm', query.astype(jnp.float32), paired[:, :, :, 0].astype(jnp.float32)) * factor
    top = lax.optimization_barrier(jnp.max(scores, axis=-1, keepdims=True))
    weights = jnp.exp(scores - top)
    probs = (weights / lax.optimization_barrier(jnp.sum(weights, axis=-1, keepdims=True))).astype(jnp.bfloat16)
    mixed = jnp.einsum('chnm,cmhd->cnhd', probs.astype(jnp.float32), paired[:, :, :, 1].astype(jnp.float32))
    mixed = mixed.astype(jnp.bfloat16).reshape(number * keys_n, heads * DH)
    projected = jnp.dot(mixed, encoder_output_weight, preferred_element_type=jnp.float32)
    return (flat.astype(jnp.float32) + projected).astype(jnp.bfloat16).reshape(number, keys_n, width)

def cross_attend(query, paired, live):
    factor = 1.0 / math.sqrt(DH)
    scores = jnp.einsum('gthd,gkhd->ghtk', query.astype(jnp.float32), paired[:, :, :, 0].astype(jnp.float32)) * factor
    mask = live[:, None, None, :]
    scores = jnp.where(mask, scores, NEG)
    top = lax.optimization_barrier(jnp.max(scores, axis=-1, keepdims=True))
    weights = jnp.where(mask, jnp.exp(scores - top), 0.0)
    total = lax.optimization_barrier(jnp.sum(weights, axis=-1, keepdims=True))
    anylive = jnp.any(live, axis=-1)[:, None, None, None]
    total = jnp.where(anylive, total, 1.0)
    probs = (weights / total).astype(jnp.bfloat16)
    mixed = jnp.einsum('ghtk,gkhd->gthd', probs.astype(jnp.float32), paired[:, :, :, 1].astype(jnp.float32))
    groups, rows, heads, size = mixed.shape
    return mixed.astype(jnp.bfloat16).reshape(groups, rows, heads * size)

def reference(hidden, gain, trace_emb, counts, offsets, w_stretch_kv, encoder_query_weight, encoder_output_weight, w_cca_q, w_cca_kv, w_cca_o):
    normed = rms_scale(hidden, gain)
    stretch_key_values = jnp.dot(normed, w_stretch_kv, preferred_element_type=jnp.float32).astype(jnp.bfloat16)
    query = jnp.dot(normed, w_cca_q, preferred_element_type=jnp.float32).astype(jnp.bfloat16)
    width = query.shape[1]
    shifted = jnp.concatenate([query, jnp.zeros((STRETCH_TOKENS - 1, width), jnp.bfloat16)], 0)
    keys_n = KNB * NLEN
    slot = jnp.arange(keys_n, dtype=jnp.int32) // NLEN

    def one_stretch(index):
        pieces = []
        for k in range(KNB):
            first = jnp.clip((index - offsets[index, k]) * STRETCH_TOKENS, 0, TOKENS - NLEN).astype(jnp.int32)
            pieces.append(lax.dynamic_slice_in_dim(trace_emb, first, NLEN, 0))
        row_count = jnp.concatenate(pieces, 0)[None]
        start_index = (index * STRETCH_TOKENS).astype(jnp.int32)
        stretch_key_value = lax.dynamic_slice_in_dim(stretch_key_values, start_index, STRETCH_TOKENS, 0)[None]
        encoded_neighbours = encode_neighbours(row_count, stretch_key_value, encoder_query_weight, encoder_output_weight)[0]
        paired = jnp.dot(encoded_neighbours, w_cca_kv, preferred_element_type=jnp.float32).astype(jnp.bfloat16)
        paired = paired.reshape(1, keys_n, HQ, 2, DH)
        qstart = (index * STRETCH_TOKENS + STRETCH_TOKENS - 1).astype(jnp.int32)
        qrows = lax.dynamic_slice_in_dim(shifted, qstart, STRETCH_TOKENS, 0).reshape(1, STRETCH_TOKENS, HQ, DH)
        live = (slot < counts[index])[None]
        return cross_attend(qrows, paired, live)[0]
    blocks = lax.map(one_stretch, jnp.arange(STRETCHES, dtype=jnp.int32))
    flat = blocks.reshape(TOKENS, width)
    attended = jnp.concatenate([jnp.zeros((STRETCH_TOKENS - 1, width), jnp.bfloat16), flat[:TOKENS - STRETCH_TOKENS + 1]], 0)
    projected = jnp.dot(attended, w_cca_o, preferred_element_type=jnp.float32)
    return (hidden.astype(jnp.float32) + projected).astype(jnp.bfloat16)
```

```python
import functools
import math

import jax
import jax.numpy as jnp
from jax import lax
from jax.experimental import pallas as pl
from jax.experimental.pallas import tpu as pltpu
from jax.sharding import PartitionSpec as P

MESH = pl.DeviceIdType.MESH
BF = jnp.bfloat16
F32 = jnp.float32
EPS = 1e-05
NEG = -1e30
FACTOR = 1.0 / math.sqrt(128)
TP = 8
PLACES = 32


def remote(src, dst, send, recv, to):
    return pltpu.make_async_remote_copy(
        src_ref=src, dst_ref=dst, send_sem=send, recv_sem=recv, device_id=to, device_id_type=MESH
    )


def dot(a, b):
    return jnp.dot(a, b, preferred_element_type=F32)


def dot_t(a, b):
    return lax.dot_general(a, b, (((1,), (1,)), ((), ())), preferred_element_type=F32)


class Here:
    def __init__(self):
        self.c = lax.axis_index("seq")
        self.t = lax.axis_index("tp")
        self.s = lax.axis_index("section")
        self.y, self.xl = self.t // 2, self.t % 2
        self.z, self.xh = self.s // 2, self.s % 2
        self.p = self.c * 16 + self.s
        c, t, s = self.c, self.t, self.s
        self.yp = (c, self.slot(1, 0), s)
        self.ym = (c, self.slot(3, 0), s)
        self.xp = (c, self.slot(0, 1), s)
        self.zp = (c, t, ((self.z + 1) % 8) * 2 + self.xh)
        self.zm = (c, t, ((self.z + 7) % 8) * 2 + self.xh)
        self.x2 = (c, t, self.z * 2 + 1 - self.xh)
        self.core = (1 - c, t, s)
        before, after = (self.p + PLACES - 1) % PLACES, (self.p + 1) % PLACES
        self.before = (before // 16, before % 16)
        self.after = (after // 16, after % 16)

    def slot(self, dy, other):
        xl = 1 - self.xl if other else self.xl
        return ((self.y + dy) % 4) * 2 + xl

    def tp_peer(self, i):
        return (self.t + i) % TP

    def at_tp(self, t):
        return (self.c, t, self.s)

    def last_before(self):
        return (self.before[0], TP - 1, self.before[1])

    def at_after(self, t):
        return (self.after[0], t, self.after[1])


class Gather:
    def __init__(self, here, region, own, send, recv, arrived):
        self.here, self.region, self.own = here, region, own
        self.send_sem, self.recv_sem, self.arrived = send, recv, arrived
        self.sent = []

    def send(self, m, to, slot, part, half=None, own=False):
        src = self.own(part) if own else self.region(slot, part, half)
        copy = remote(src, self.region(slot, part, half), self.send_sem.at[m], self.recv_sem.at[m], to)
        copy.start()
        self.sent.append(copy)

    def wait(self, m, slot, part, half=None):
        ref = self.region(slot, part, half)
        remote(ref, ref, self.send_sem.at[m], self.recv_sem.at[m], self.here.xp).wait_recv()

    def begin(self, part):
        h = self.here
        me = h.t
        if part == 0:
            self.send(0, h.xp, me, 0, own=True)
            self.send(1, h.yp, me, 0, own=True)
            self.send(2, h.ym, me, 0, own=True)
        else:
            self.send(4, h.yp, me, 1, own=True)
            self.send(5, h.ym, me, 1, own=True)
            self.send(3, h.xp, me, 1, own=True)

    def steps(self):
        h = self.here
        slot = h.slot
        self.wait(0, slot(0, 1), 0)
        self.send(6, h.yp, slot(0, 1), 0)
        self.send(7, h.ym, slot(0, 1), 0)
        self.arrived(slot(0, 1), 0, 0)
        yield
        self.wait(4, slot(3, 0), 1)
        self.send(12, h.xp, slot(3, 0), 1)
        self.send(14, h.yp, slot(3, 0), 1, 0)
        self.arrived(slot(3, 0), 1, 1)
        yield
        self.wait(5, slot(1, 0), 1)
        self.send(13, h.xp, slot(1, 0), 1)
        self.send(15, h.ym, slot(1, 0), 1, 1)
        self.arrived(slot(1, 0), 1, 2)
        yield
        self.wait(1, slot(3, 0), 0)
        self.send(8, h.yp, slot(3, 0), 0, 0)
        self.arrived(slot(3, 0), 0, 3)
        yield
        self.wait(2, slot(1, 0), 0)
        self.send(9, h.ym, slot(1, 0), 0, 1)
        self.arrived(slot(1, 0), 0, 4)
        yield
        self.wait(3, slot(0, 1), 1)
        self.arrived(slot(0, 1), 1, 5)
        yield
        self.wait(14, slot(2, 0), 1, 0)
        self.send(16, h.xp, slot(2, 0), 1, 0)
        self.wait(15, slot(2, 0), 1, 1)
        self.send(17, h.xp, slot(2, 0), 1, 1)
        self.arrived(slot(2, 0), 1, 6)
        yield
        self.wait(6, slot(3, 1), 0)
        self.send(10, h.yp, slot(3, 1), 0, 0)
        self.arrived(slot(3, 1), 0, 7)
        yield
        self.wait(7, slot(1, 1), 0)
        self.send(11, h.ym, slot(1, 1), 0, 1)
        self.arrived(slot(1, 1), 0, 8)
        yield
        self.wait(8, slot(2, 0), 0, 0)
        self.wait(9, slot(2, 0), 0, 1)
        self.arrived(slot(2, 0), 0, 9)
        yield
        self.wait(12, slot(3, 1), 1)
        self.arrived(slot(3, 1), 1, 10)
        yield
        self.wait(13, slot(1, 1), 1)
        self.arrived(slot(1, 1), 1, 11)
        yield
        self.wait(10, slot(2, 1), 0, 0)
        self.wait(11, slot(2, 1), 0, 1)
        self.arrived(slot(2, 1), 0, 12)
        yield
        self.wait(16, slot(2, 1), 1, 0)
        self.wait(17, slot(2, 1), 1, 1)
        self.arrived(slot(2, 1), 1, 13)

    def order(self):
        s = self.here.slot
        return [
            (s(0, 1), 0), (s(3, 0), 1), (s(1, 0), 1), (s(3, 0), 0), (s(1, 0), 0), (s(0, 1), 1), (s(2, 0), 1),
            (s(3, 1), 0), (s(1, 1), 0), (s(2, 0), 0), (s(3, 1), 1), (s(1, 1), 1), (s(2, 1), 0), (s(2, 1), 1),
        ]

    def finish(self):
        for copy in self.sent:
            copy.wait_send()


class Ring:
    OFFSET = [0, 7, 1, 6, 2, 5, 3, 4]

    def __init__(self, here, region, sems, flip):
        self.here, self.region, self.flip = here, region, flip
        self.send_sem, self.recv_sem, self.core_send, self.core_recv = sems
        self.sent = []

    def push(self, way, r):
        h = self.here
        z = (h.z + (8 - r if way == 0 else r)) % 8
        ref = self.region(z, h.c)
        m = way * 4 + r
        copy = remote(ref, ref, self.send_sem.at[m], self.recv_sem.at[m], h.zp if way == 0 else h.zm)
        copy.start()
        self.sent.append(copy)

    def share(self, k):
        h = self.here
        ref = self.region((h.z + self.dz(k)) % 8, h.c)
        copy = remote(ref, ref, self.core_send.at[k], self.core_recv.at[k], h.core)
        copy.start()
        self.sent.append(copy)

    def dz(self, k):
        return self.OFFSET[k] if not self.flip else (8 - self.OFFSET[k]) % 8

    def wait(self, way, r, k):
        h = self.here
        ref = self.region((h.z + self.dz(k)) % 8, h.c)
        m = way * 4 + r
        remote(ref, ref, self.send_sem.at[m], self.recv_sem.at[m], h.zp).wait_recv()

    def steps(self):
        first, second = (1, 0) if self.flip else (0, 1)
        self.push(first, 0)
        self.push(second, 0)
        self.share(0)
        yield
        for r in range(3):
            self.wait(first, r, 1 + 2 * r)
            self.push(first, r + 1)
            self.share(1 + 2 * r)
            self.wait(second, r, 2 + 2 * r)
            if r < 2:
                self.push(second, r + 1)
            self.share(2 + 2 * r)
            yield
        self.wait(first, 3, 7)
        self.share(7)
        yield

    def collect(self):
        h = self.here
        for k in range(8):
            ref = self.region((h.z + self.dz(k)) % 8, 1 - h.c)
            remote(ref, ref, self.core_send.at[k], self.core_recv.at[k], h.core).wait_recv()

    def finish(self):
        for copy in self.sent:
            copy.wait_send()


def advance(steps, n=1):
    for _ in range(n):
        next(steps, None)


def kernel(
    hidden, gain, trace, counts, offsets, w_skv, w_eq, w_eo, w_cq, w_ckv, w_co, out,
    hid, wproj, acc, ssq, kv_s, q_s, tr, picked, rows, enc_w, wck, woc, kvx, qx, qh, eq, ea, enc,
    att_own, attg, tail, attb,
    local, h_send, h_recv, k_send, k_recv, a_send, a_recv, kc_send, kc_recv,
    x_send, x_recv, tr_ss, tr_rs, tr_cs, tr_cr, e_ss, e_rs, e_cs, e_cr, o_ss, o_rs, o_cs, o_cr,
    p_send, p_recv, halo_send, halo_recv, tail_send, tail_recv,
):
    h = Here()
    c, t, s, z, xh, p = h.c, h.t, h.s, h.z, h.xh, h.p
    is_last = t == TP - 1

    barrier = pltpu.get_barrier_semaphore()
    greet = [h.at_tp(h.tp_peer(i)) for i in range(1, TP)]
    greet += [h.zp, h.zm, h.x2, h.core, h.last_before()]
    for device in greet:
        pl.semaphore_signal(barrier, inc=1, device_id=device, device_id_type=MESH)

    @pl.when(is_last)
    def _():
        for other in range(TP):
            pl.semaphore_signal(barrier, inc=1, device_id=h.at_after(other), device_id_type=MESH)

    pl.semaphore_wait(barrier, len(greet) + TP * (t // (TP - 1)))

    started = []

    def bring(src, dst, i):
        copy = pltpu.make_async_copy(src, dst, local.at[i])
        copy.start()
        return copy

    def hid_region(slot, part, half):
        if half is None:
            return hid.at[slot, pl.ds(part * 256, 256)]
        return hid.at[slot, pl.ds(part * 256 + half * 128, 128)]

    first = []

    def project(slot, part, index):
        here = pl.ds(part * 256, 256)
        wide = hid[slot, here, :].astype(F32)
        squares = jnp.sum(wide * wide, axis=-1, keepdims=True)
        scaled = (wide * gain[slot]).astype(BF)
        w = wproj[pl.ds(pl.multiple_of(slot * 512, 512), 512), :]
        product = dot(scaled, w)
        if index is None:
            ssq[here, :] = squares
            acc[here, :] = product
        else:
            ssq[here, :] += squares
            acc[here, :] += product

    gather_h = Gather(
        h, hid_region, lambda part: hidden.at[pl.ds(part * 256, 256)], h_send, h_recv, project
    )
    gather_h.begin(0)
    gather_h.begin(1)

    mine = pl.ds(p * 8, 8)
    other = pl.ds((p + 1 - 2 * xh) * 8, 8)
    trace_x2 = remote(trace, tr.at[mine], x_send.at[0], x_recv.at[0], h.x2)
    trace_x2.start()
    own_trace = bring(trace, tr.at[mine], 0)
    own_hid = bring(hidden, hid.at[t], 1)
    own_skv = bring(w_skv, wproj.at[:, pl.ds(0, 256)], 2)
    own_cq = bring(w_cq, wproj.at[:, pl.ds(256, 256)], 3)
    halves = pl.ds(c * 32, 32)
    own_eq = bring(w_eq.at[halves], enc_w.at[0, s, c], 4)
    own_eo = bring(w_eo.at[halves], enc_w.at[1, s, c], 5)
    own_ckv = bring(w_ckv, wck.at[t], 6)
    slice_rows = pl.ds(z * 32 + c * 16, 16)
    own_co = bring(
        w_co.at[slice_rows, pl.ds(pl.multiple_of(t * 512, 512), 512)], woc.at[t, z * 2 + c], 7
    )

    trace_in = remote(tr.at[other], tr.at[other], x_send.at[0], x_recv.at[0], h.x2)
    own_trace.wait()
    trace_in.wait_recv()
    ring_t = Ring(
        h, lambda zz, cc: tr.at[pl.ds((cc * 16 + zz * 2) * 8, 16)],
        (tr_ss, tr_rs, tr_cs, tr_cr), False,
    )
    steps_t = ring_t.steps()
    advance(steps_t)

    eq_x2 = remote(w_eq.at[halves], enc_w.at[0, s, c], x_send.at[1], x_recv.at[1], h.x2)
    eo_x2 = remote(w_eo.at[halves], enc_w.at[1, s, c], x_send.at[2], x_recv.at[2], h.x2)
    eq_x2.start()
    eo_x2.start()
    pushes = []
    for i in range(1, TP):
        to = h.tp_peer(i)
        copy = remote(
            w_co.at[slice_rows, pl.ds(pl.multiple_of(to * 512, 512), 512)], woc.at[t, z * 2 + c],
            p_send.at[0, i], p_recv.at[0, i], h.at_tp(to),
        )
        copy.start()
        pushes.append(copy)

    own_hid.wait()
    own_skv.wait()
    own_cq.wait()
    project(t, 0, None)
    project(t, 1, None)

    steps_h = gather_h.steps()
    advance(steps_h, 3)
    advance(steps_t)
    advance(steps_h, 3)
    advance(steps_t)
    own_eq.wait()
    own_eo.wait()
    s_other = z * 2 + 1 - xh
    for w in range(2):
        ref = enc_w.at[w, s_other, c]
        remote(ref, ref, x_send.at[1 + w], x_recv.at[1 + w], h.x2).wait_recv()
    ring_e = Ring(
        h, lambda zz, cc: enc_w.at[:, pl.ds(zz * 2, 2), cc], (e_ss, e_rs, e_cs, e_cr), True
    )
    steps_e = ring_e.steps()
    advance(steps_h, 2)
    advance(steps_t)
    advance(steps_e)
    advance(steps_h, 3)
    advance(steps_t)
    advance(steps_e)
    advance(steps_h, 4)

    inverse = lax.rsqrt(ssq[...] * (1.0 / 4096) + EPS)
    projected = (acc[...] * inverse).astype(BF)
    kv_s[...] = projected[:, :256]
    q_s[0:512, :] = projected[:, 256:]
    q_s[512:576, :] = jnp.zeros((64, 256), BF)
    for i in range(1, TP):
        to = h.tp_peer(i)
        copy = remote(
            kv_s.at[pl.ds(pl.multiple_of(to * 64, 64), 64)], kvx.at[t],
            p_send.at[1, i], p_recv.at[1, i], h.at_tp(to),
        )
        copy.start()
        pushes.append(copy)
    kvx[t] = kv_s[pl.ds(pl.multiple_of(t * 64, 64), 64), :]

    ring_t.collect()

    def pick(owner):
        for k in range(4):
            at = p * 8 + owner - offsets[owner, k]
            at = jnp.minimum(jnp.maximum(at, 0), 254)
            picked[owner, 128 * k : 128 * k + 64, :] = tr[at]
            picked[owner, 128 * k + 64 : 128 * k + 128, :] = tr[at + 1]

    columns = pl.ds(pl.multiple_of(t * 128, 128), 128)
    for i in range(1, TP):
        to = h.tp_peer(i)
        pick(to)
        copy = remote(
            picked.at[to], rows.at[:, columns], p_send.at[2, i], p_recv.at[2, i], h.at_tp(to)
        )
        copy.start()
        pushes.append(copy)
    pick(t)
    rows[:, columns] = picked[t]

    for i in range(1, TP):
        to = h.tp_peer(i)
        copy = remote(
            q_s.at[pl.ds(pl.multiple_of(to * 64 + 48, 16), 80)], qx.at[t],
            p_send.at[3, i], p_recv.at[3, i], h.at_tp(to),
        )
        copy.start()
        pushes.append(copy)
    qx[t] = q_s[pl.ds(pl.multiple_of(t * 64 + 48, 16), 80), :]
    halo = remote(q_s.at[pl.ds(0, 64)], qh.at[t], halo_send.at[0], halo_recv.at[t], h.last_before())
    halo.start()
    pushes.append(halo)

    advance(steps_e)

    def wck_region(slot, part, half):
        base = c * 512 + part * 256
        if half is None:
            return wck.at[slot, pl.ds(base, 256)]
        return wck.at[slot, pl.ds(base + half * 128, 128)]

    shared = []

    def share(slot, part, index):
        ref = wck_region(slot, part, None)
        copy = remote(ref, ref, kc_send.at[index], kc_recv.at[index], h.core)
        copy.start()
        shared.append(copy)

    own_ckv.wait()
    gather_k = Gather(
        h, wck_region, lambda part: wck.at[t, pl.ds(c * 512 + part * 256, 256)], k_send, k_recv, share
    )
    gather_k.begin(0)
    gather_k.begin(1)
    steps_k = gather_k.steps()

    own_co.wait()
    for i in range(1, TP):
        ref = woc.at[h.tp_peer(TP - i), z * 2 + c]
        remote(ref, ref, p_send.at[0, i], p_recv.at[0, i], h.core).wait_recv()
    ring_o = Ring(h, lambda zz, cc: woc.at[:, zz * 2 + cc], (o_ss, o_rs, o_cs, o_cr), False)
    steps_o = ring_o.steps()

    advance(steps_e, 2)
    advance(steps_o)
    for i in range(1, TP):
        came = h.tp_peer(TP - i)
        ref = rows.at[:, pl.ds(pl.multiple_of(came * 128, 128), 128)]
        remote(ref, ref, p_send.at[2, i], p_recv.at[2, i], h.core).wait_recv()
    ring_e.collect()
    advance(steps_k, 2)

    for n in range(4):
        cols = slice(256 * n, 256 * (n + 1))
        eq[:, cols] = dot(rows[...], enc_w[0, :, :, :, cols].reshape(1024, 256)).astype(BF)
    for i in range(1, TP):
        came = h.tp_peer(TP - i)
        ref = kvx.at[came]
        remote(ref, ref, p_send.at[1, i], p_recv.at[1, i], h.core).wait_recv()
    advance(steps_k, 1)
    for e in range(8):
        cols = slice(128 * e, 128 * (e + 1))
        scores = dot_t(eq[:, cols], kvx[e, :, :128]) * FACTOR
        top = jnp.max(scores, axis=-1, keepdims=True)
        weights = jnp.exp(scores - top)
        probs = (weights / jnp.sum(weights, axis=-1, keepdims=True)).astype(BF)
        ea[:, cols] = dot(probs, kvx[e, :, 128:]).astype(BF)
        advance(steps_k, 1)
        if e % 2:
            advance(steps_o)
    for n in range(4):
        cols = slice(256 * n, 256 * (n + 1))
        update = dot(ea[...], enc_w[1, :, :, :, cols].reshape(1024, 256))
        enc[:, cols] = (rows[:, cols].astype(F32) + update).astype(BF)
    advance(steps_k, 3)

    for i in range(1, TP):
        came = h.tp_peer(TP - i)
        ref = qx.at[came]
        remote(ref, ref, p_send.at[3, i], p_recv.at[3, i], h.core).wait_recv()

    @pl.when(is_last)
    def _():
        for j in range(TP):
            ref = qh.at[j]
            remote(ref, ref, halo_send.at[0], halo_recv.at[j], h.core).wait_recv()
            qx[j, 16:80, :] = qh[j]

    for index, (slot, part) in enumerate(gather_k.order()):
        ref = wck.at[slot, pl.ds((1 - c) * 512 + part * 256, 256)]
        remote(ref, ref, kc_send.at[index], kc_recv.at[index], h.core).wait_recv()

    live_keys = counts[t] * 128
    lane = lax.broadcasted_iota(jnp.int32, (80, 512), 1)
    mask = lane < live_keys
    row = lax.broadcasted_iota(jnp.int32, (80, 128), 0)
    keep = (row >= 15) & (row < 79)

    def att_region(slot, part, half):
        if half is None:
            return attg.at[slot, :, pl.ds(part * 1024, 1024)]
        return attg.at[slot, :, pl.ds(part * 1024 + half * 512, 512)]

    gather_a = Gather(
        h, att_region, lambda part: att_own.at[:, pl.ds(part * 1024, 1024)], a_send, a_recv,
        lambda slot, part, index: None,
    )
    for j in range(TP):
        pair = dot(enc[...], wck[j]).astype(BF)
        for half in range(2):
            key = pair[:, 256 * half : 256 * half + 128]
            value = pair[:, 256 * half + 128 : 256 * half + 256]
            query = qx[j, :, 128 * half : 128 * half + 128]
            scores = jnp.where(mask, dot_t(query, key) * FACTOR, NEG)
            top = jnp.max(scores, axis=-1, keepdims=True)
            weights = jnp.where(mask, jnp.exp(scores - top), 0.0)
            total = jnp.sum(weights, axis=-1, keepdims=True)
            total = jnp.where(total > 0.0, total, 1.0)
            probs = (weights / total).astype(BF)
            mixed = jnp.where(keep, dot(probs, value), 0.0).astype(BF)
            at = 256 * j + 128 * half
            att_own[:, at : at + 128] = mixed
        if j == 3:
            gather_a.begin(0)
    gather_a.begin(1)

    @pl.when(is_last)
    def _():
        for j in range(TP):
            remote(
                att_own.at[pl.ds(16, 64), pl.ds(256 * j, 256)], tail.at[j],
                tail_send.at[j], tail_recv.at[0], h.at_after(j),
            ).start()

    steps_a = gather_a.steps()
    advance(steps_a, 3)
    remote(tail.at[t], tail.at[t], tail_send.at[0], tail_recv.at[0], h.core).wait_recv()
    for i in range(1, TP):
        copy = remote(tail.at[t], tail.at[t], p_send.at[4, i], p_recv.at[4, i], h.at_tp(h.tp_peer(i)))
        copy.start()
        pushes.append(copy)
    advance(steps_a, 11)
    attg[t] = att_own[...]
    for i in range(1, TP):
        ref = tail.at[h.tp_peer(TP - i)]
        remote(ref, ref, p_send.at[4, i], p_recv.at[4, i], h.core).wait_recv()
    ring_o.collect()

    for j in range(TP):
        attb[0:64, 256 * j : 256 * (j + 1)] = jnp.where(p > 0, tail[j].astype(F32), 0.0).astype(BF)
    for v in range(TP):
        if v:
            attb[64 * v : 64 * v + 64, :] = attg[v - 1, 16:80, :]
        attb[64 * v + 48 : 64 * v + 64, :] += attg[v, 0:16, :]
    for n in range(2):
        cols = slice(256 * n, 256 * (n + 1))
        update = dot(attb[...], woc[:, :, :, cols].reshape(2048, 256))
        out[:, cols] = (hid[t, :, cols].astype(F32) + update).astype(BF)

    gather_h.finish()
    gather_k.finish()
    gather_a.finish()
    ring_t.finish()
    ring_e.finish()
    ring_o.finish()
    trace_x2.wait_send()
    eq_x2.wait_send()
    eo_x2.wait_send()
    for copy in shared + pushes:
        copy.wait_send()

    @pl.when(is_last)
    def _():
        for j in range(TP):
            remote(
                att_own.at[pl.ds(16, 64), pl.ds(256 * j, 256)], tail.at[j],
                tail_send.at[j], tail_recv.at[0], h.at_after(j),
            ).wait_send()


def body(hidden, gain, trace, counts, offsets, w_skv, w_eq, w_eo, w_cq, w_ckv, w_co):
    any_ = pl.BlockSpec(memory_space=pl.ANY)
    vmem = pl.BlockSpec(memory_space=pltpu.VMEM)
    smem = pl.BlockSpec(memory_space=pltpu.SMEM)
    dma = pltpu.SemaphoreType.DMA
    v = pltpu.VMEM
    scratch = [
        v((8, 512, 512), BF),
        v((4096, 512), BF),
        v((512, 512), F32),
        v((512, 1), F32),
        v((512, 256), BF),
        v((576, 256), BF),
        v((256, 64, 128), BF),
        v((8, 512, 128), BF),
        v((512, 1024), BF),
        v((2, 16, 2, 32, 1024), BF),
        v((8, 1024, 512), BF),
        v((8, 16, 16, 512), BF),
        v((8, 64, 256), BF),
        v((8, 80, 256), BF),
        v((8, 64, 256), BF),
        v((512, 1024), BF),
        v((512, 1024), BF),
        v((512, 1024), BF),
        v((80, 2048), BF),
        v((8, 80, 2048), BF),
        v((8, 64, 256), BF),
        v((512, 2048), BF),
        dma((8,)),
        dma((18,)), dma((18,)), dma((18,)), dma((18,)), dma((18,)), dma((18,)), dma((14,)), dma((14,)),
        dma((3,)), dma((3,)),
        dma((8,)), dma((8,)), dma((8,)), dma((8,)),
        dma((8,)), dma((8,)), dma((8,)), dma((8,)),
        dma((8,)), dma((8,)), dma((8,)), dma((8,)),
        dma((5, 8)), dma((5, 8)),
        dma((1,)), dma((8,)), dma((8,)), dma((1,)),
    ]
    return pl.pallas_call(
        kernel,
        out_shape=jax.ShapeDtypeStruct((512, 512), BF),
        in_specs=[any_, vmem, any_, smem, smem, any_, any_, any_, any_, any_, any_],
        out_specs=vmem,
        scratch_shapes=scratch,
        compiler_params=pltpu.CompilerParams(
            collective_id=0, has_side_effects=True, vmem_limit_bytes=58 << 20
        ),
        cost_estimate=pl.CostEstimate(flops=11_000_000_000, bytes_accessed=14_000_000, transcendentals=1_000_000),
    )(
        hidden, gain.astype(F32).reshape(8, 1, 512), trace.reshape(8, 64, 128), counts, offsets,
        w_skv, w_eq, w_eo, w_cq, w_ckv, w_co,
    )


def solution(mesh):
    place = ("seq", "section")
    in_specs = (
        P(place, "tp"), P(), P(place, "tp"), P(place), P(place, None), P(None, "tp"),
        P("section", None), P("section", None), P(None, "tp"), P(None, "tp"), P("tp", None),
    )
    return jax.shard_map(body, mesh=mesh, in_specs=in_specs, out_specs=P(place, "tp"), check_vma=False)
```

```python
import functools
import math

import jax
import jax.numpy as jnp
from jax import lax
from jax.experimental import pallas as pl
from jax.experimental.pallas import tpu as pltpu
from jax.sharding import PartitionSpec as P

MESH = pl.DeviceIdType.MESH
BF = jnp.bfloat16
F32 = jnp.float32
EPS = 1e-05
NEG = -1e30
FACTOR = 1.0 / math.sqrt(128)
TP = 8
PLACES = 32


def remote(src, dst, send, recv, to):
    return pltpu.make_async_remote_copy(
        src_ref=src, dst_ref=dst, send_sem=send, recv_sem=recv, device_id=to, device_id_type=MESH
    )


def dot(a, b):
    return jnp.dot(a, b, preferred_element_type=F32)


def dot_t(a, b):
    return lax.dot_general(a, b, (((1,), (1,)), ((), ())), preferred_element_type=F32)


class Here:
    def __init__(self):
        self.c = lax.axis_index("seq")
        self.t = lax.axis_index("tp")
        self.s = lax.axis_index("section")
        self.y, self.xl = self.t // 2, self.t % 2
        self.z, self.xh = self.s // 2, self.s % 2
        self.p = self.c * 16 + self.s
        c, t, s = self.c, self.t, self.s
        self.yp = (c, self.slot(1, 0), s)
        self.ym = (c, self.slot(3, 0), s)
        self.xp = (c, self.slot(0, 1), s)
        self.zp = (c, t, ((self.z + 1) % 8) * 2 + self.xh)
        self.zm = (c, t, ((self.z + 7) % 8) * 2 + self.xh)
        self.x2 = (c, t, self.z * 2 + 1 - self.xh)
        self.xo = (c, self.slot(0, 1), self.z * 2 + 1 - self.xh)
        self.core = (1 - c, t, s)
        before, after = (self.p + PLACES - 1) % PLACES, (self.p + 1) % PLACES
        self.before = (before // 16, before % 16)
        self.after = (after // 16, after % 16)

    def slot(self, dy, other):
        xl = 1 - self.xl if other else self.xl
        return ((self.y + dy) % 4) * 2 + xl

    def tp_peer(self, i):
        return (self.t + i) % TP

    def any_copy(self, dy, other):
        return (self.c, self.slot(dy, other), self.z * 2 + (1 - self.xh if other else self.xh))

    def at_tp(self, t):
        return (self.c, t, self.s)

    def last_before(self):
        return (self.before[0], TP - 1, self.before[1])

    def at_after(self, t):
        return (self.after[0], t, self.after[1])


class Gather:
    def __init__(self, here, region, own, send, recv, arrived, xp):
        self.here, self.region, self.own, self.xp = here, region, own, xp
        self.send_sem, self.recv_sem, self.arrived = send, recv, arrived
        self.sent = []

    def send(self, m, to, slot, part, half=None, own=False):
        src = self.own(part) if own else self.region(slot, part, half)
        copy = remote(src, self.region(slot, part, half), self.send_sem.at[m], self.recv_sem.at[m], to)
        copy.start()
        self.sent.append(copy)

    def wait(self, m, slot, part, half=None):
        ref = self.region(slot, part, half)
        remote(ref, ref, self.send_sem.at[m], self.recv_sem.at[m], self.xp).wait_recv()

    def begin(self, part):
        if part == 0:
            self.begin_x(0)
            self.begin_y(0)
        else:
            self.begin_y(1)
            self.begin_x(1)

    def begin_x(self, part):
        self.send(3 * part, self.xp, self.here.t, part, own=True)

    def begin_y(self, part):
        h = self.here
        self.send(3 * part + 1, h.yp, h.t, part, own=True)
        self.send(3 * part + 2, h.ym, h.t, part, own=True)

    def steps(self):
        h = self.here
        slot = h.slot
        self.wait(0, slot(0, 1), 0)
        self.send(6, h.yp, slot(0, 1), 0)
        self.send(7, h.ym, slot(0, 1), 0)
        self.arrived(slot(0, 1), 0, 0)
        yield
        self.wait(4, slot(3, 0), 1)
        self.send(12, self.xp, slot(3, 0), 1)
        self.send(14, h.yp, slot(3, 0), 1, 0)
        self.arrived(slot(3, 0), 1, 1)
        yield
        self.wait(5, slot(1, 0), 1)
        self.send(13, self.xp, slot(1, 0), 1)
        self.send(15, h.ym, slot(1, 0), 1, 1)
        self.arrived(slot(1, 0), 1, 2)
        yield
        self.wait(1, slot(3, 0), 0)
        self.send(8, h.yp, slot(3, 0), 0, 0)
        self.arrived(slot(3, 0), 0, 3)
        yield
        self.wait(2, slot(1, 0), 0)
        self.send(9, h.ym, slot(1, 0), 0, 1)
        self.arrived(slot(1, 0), 0, 4)
        yield
        self.wait(3, slot(0, 1), 1)
        self.arrived(slot(0, 1), 1, 5)
        yield
        self.wait(14, slot(2, 0), 1, 0)
        self.send(16, self.xp, slot(2, 0), 1, 0)
        self.wait(15, slot(2, 0), 1, 1)
        self.send(17, self.xp, slot(2, 0), 1, 1)
        self.arrived(slot(2, 0), 1, 6)
        yield
        self.wait(6, slot(3, 1), 0)
        self.send(10, h.yp, slot(3, 1), 0, 0)
        self.arrived(slot(3, 1), 0, 7)
        yield
        self.wait(7, slot(1, 1), 0)
        self.send(11, h.ym, slot(1, 1), 0, 1)
        self.arrived(slot(1, 1), 0, 8)
        yield
        self.wait(8, slot(2, 0), 0, 0)
        self.wait(9, slot(2, 0), 0, 1)
        self.arrived(slot(2, 0), 0, 9)
        yield
        self.wait(12, slot(3, 1), 1)
        self.arrived(slot(3, 1), 1, 10)
        yield
        self.wait(13, slot(1, 1), 1)
        self.arrived(slot(1, 1), 1, 11)
        yield
        self.wait(10, slot(2, 1), 0, 0)
        self.wait(11, slot(2, 1), 0, 1)
        self.arrived(slot(2, 1), 0, 12)
        yield
        self.wait(16, slot(2, 1), 1, 0)
        self.wait(17, slot(2, 1), 1, 1)
        self.arrived(slot(2, 1), 1, 13)

    def order(self):
        s = self.here.slot
        return [
            (s(0, 1), 0), (s(3, 0), 1), (s(1, 0), 1), (s(3, 0), 0), (s(1, 0), 0), (s(0, 1), 1), (s(2, 0), 1),
            (s(3, 1), 0), (s(1, 1), 0), (s(2, 0), 0), (s(3, 1), 1), (s(1, 1), 1), (s(2, 1), 0), (s(2, 1), 1),
        ]

    def finish(self):
        for copy in self.sent:
            copy.wait_send()


class Ring:
    OFFSET = [0, 7, 1, 6, 2, 5, 3, 4]

    def __init__(self, here, region, sems, flip):
        self.here, self.region, self.flip = here, region, flip
        self.send_sem, self.recv_sem, self.core_send, self.core_recv = sems
        self.sent = []

    def push(self, way, r):
        h = self.here
        z = (h.z + (8 - r if way == 0 else r)) % 8
        ref = self.region(z, h.c)
        m = way * 4 + r
        copy = remote(ref, ref, self.send_sem.at[m], self.recv_sem.at[m], h.zp if way == 0 else h.zm)
        copy.start()
        self.sent.append(copy)

    def share(self, k):
        h = self.here
        ref = self.region((h.z + self.dz(k)) % 8, h.c)
        copy = remote(ref, ref, self.core_send.at[k], self.core_recv.at[k], h.core)
        copy.start()
        self.sent.append(copy)

    def dz(self, k):
        return self.OFFSET[k] if not self.flip else (8 - self.OFFSET[k]) % 8

    def wait(self, way, r, k):
        h = self.here
        ref = self.region((h.z + self.dz(k)) % 8, h.c)
        m = way * 4 + r
        remote(ref, ref, self.send_sem.at[m], self.recv_sem.at[m], h.zp).wait_recv()

    def steps(self):
        first, second = (1, 0) if self.flip else (0, 1)
        self.push(first, 0)
        self.push(second, 0)
        self.share(0)
        yield
        for r in range(3):
            self.wait(first, r, 1 + 2 * r)
            self.push(first, r + 1)
            self.share(1 + 2 * r)
            self.wait(second, r, 2 + 2 * r)
            if r < 2:
                self.push(second, r + 1)
            self.share(2 + 2 * r)
            yield
        self.wait(first, 3, 7)
        self.share(7)
        yield

    def collect(self):
        h = self.here
        for k in range(8):
            ref = self.region((h.z + self.dz(k)) % 8, 1 - h.c)
            remote(ref, ref, self.core_send.at[k], self.core_recv.at[k], h.core).wait_recv()

    def finish(self):
        for copy in self.sent:
            copy.wait_send()


def advance(steps, n=1):
    for _ in range(n):
        next(steps, None)


def kernel(
    hidden, gain, trace, counts, offsets, w_skv, w_eq, w_eo, w_cq, w_ckv, w_co, out,
    hid, wproj, acc, ssq, kv_s, q_s, tr, picked, rows, enc_w, wck, woc, kvx, qx, qh, eq, ea, enc,
    att_own, attg, tail, attb,
    local, h_send, h_recv, k_send, k_recv, a_send, a_recv, kc_send, kc_recv,
    x_send, x_recv, r_ss, r_rs, r_cs, r_cr,
    p_send, p_recv, halo_send, halo_recv, tail_send, tail_recv,
):
    h = Here()
    c, t, s, z, xh, p = h.c, h.t, h.s, h.z, h.xh, h.p
    is_last = t == TP - 1

    barrier = pltpu.get_barrier_semaphore()
    greet = [h.at_tp(h.tp_peer(i)) for i in range(1, TP)]
    greet += [h.any_copy(dy, 1) for dy in range(4)]
    greet += [h.zp, h.zm, h.x2, h.core, h.last_before()]
    for device in greet:
        pl.semaphore_signal(barrier, inc=1, device_id=device, device_id_type=MESH)

    @pl.when(is_last)
    def _():
        for other in range(TP):
            pl.semaphore_signal(barrier, inc=1, device_id=h.at_after(other), device_id_type=MESH)

    pl.semaphore_wait(barrier, len(greet) + TP * (t // (TP - 1)))

    pushes = []

    def push(src, dst, send, recv, to):
        copy = remote(src, dst, send, recv, to)
        copy.start()
        pushes.append(copy)

    def came(ref, recv):
        remote(ref, ref, p_send.at[0, 0], recv, h.core).wait_recv()

    def bring(src, dst, i):
        copy = pltpu.make_async_copy(src, dst, local.at[i])
        copy.start()
        return copy

    def project(slot, part, index):
        here = pl.ds(part * 256, 256)
        wide = hid[slot, here, :].astype(F32)
        squares = jnp.sum(wide * wide, axis=-1, keepdims=True)
        scaled = (wide * gain[slot]).astype(BF)
        w = wproj[pl.ds(pl.multiple_of(slot * 512, 512), 512), :]
        product = dot(scaled, w)
        if index is None:
            ssq[here, :] = squares
            acc[here, :] = product
        else:
            ssq[here, :] += squares
            acc[here, :] += product

    def hid_gather(i):
        def region(slot, part, half):
            base = part * 256 + i * 128
            if half is None:
                return hid.at[slot, pl.ds(base, 128)]
            return hid.at[slot, pl.ds(base + half * 64, 64)]

        def own(part):
            return hidden.at[pl.ds(part * 256 + i * 128, 128)]

        def arrived(slot, part, index):
            if i == 1:
                project(slot, part, index)

        return Gather(h, region, own, h_send.at[i], h_recv.at[i], arrived, h.xp)

    gather_h = [hid_gather(0), hid_gather(1)]
    for g in gather_h:
        g.begin(0)
        g.begin(1)
    steps_h = [g.steps() for g in gather_h]

    mine = pl.ds(p * 8, 8)
    halves = pl.ds(c * 32, 32)
    push(trace, tr.at[mine], x_send.at[0], x_recv.at[0], h.x2)
    own_trace = bring(trace, tr.at[mine], 0)
    own_hid = bring(hidden, hid.at[t], 1)
    own_skv = bring(w_skv, wproj.at[:, pl.ds(0, 256)], 2)
    own_cq = bring(w_cq, wproj.at[:, pl.ds(256, 256)], 3)
    own_eq = bring(w_eq.at[halves], enc_w.at[0, s, c], 4)
    own_eo = bring(w_eo.at[halves], enc_w.at[1, s, c], 5)
    own_ckv = [bring(w_ckv.at[pl.ds(512 * i, 256)], wck.at[t, pl.ds(512 * i, 256)], 6 + i) for i in range(2)]
    ck_rows = pl.ds(c * 512 + 256 + z * 32, 32)
    own_ckv.append(bring(w_ckv.at[ck_rows], wck.at[t, ck_rows], 8))
    co_rows = pl.ds(z * 32 + c * 16, 16)
    own_co = bring(w_co.at[co_rows, pl.ds(pl.multiple_of(t * 512, 512), 512)], woc.at[t, z * 2 + c], 9)

    def ring(i, region, flip):
        return Ring(h, region, (r_ss.at[i], r_rs.at[i], r_cs.at[i], r_cr.at[i]), flip)

    def trace_ring(i, sel):
        return ring(i, lambda zz, cc: tr.at[pl.ds((cc * 16 + zz * 2 + sel) * 8, 8)], bool(i % 2))

    def enc_ring(i, sel):
        return ring(i, lambda zz, cc: enc_w.at[:, zz * 2 + sel, cc], bool(i % 2))

    def ckv_ring(i):
        return ring(
            i, lambda zz, cc: wck.at[pl.ds(4 * (i % 2), 4), pl.ds(cc * 512 + 256 + zz * 32, 32)], bool(i % 2)
        )

    def co_ring(i):
        return ring(i, lambda zz, cc: woc.at[pl.ds(4 * (i % 2), 4), zz * 2 + cc], bool(i % 2))

    rings_t = [trace_ring(0, xh), trace_ring(1, 1 - xh)]
    rings_e = [enc_ring(2, xh), enc_ring(3, 1 - xh)]
    rings_k = [ckv_ring(4), ckv_ring(5)]
    rings_o = [co_ring(6), co_ring(7)]
    rings = rings_t + rings_e + rings_k + rings_o
    steps_t, steps_e, steps_k2, steps_o = (
        [r.steps() for r in group] for group in (rings_t, rings_e, rings_k, rings_o)
    )

    own_trace.wait()
    advance(steps_t[0])
    came(tr.at[pl.ds((p + 1 - 2 * xh) * 8, 8)], x_recv.at[0])
    advance(steps_t[1])

    def wck_region(slot, part, half):
        base = c * 512 + part * 128
        if half is None:
            return wck.at[slot, pl.ds(base, 128)]
        return wck.at[slot, pl.ds(base + half * 64, 64)]

    def share(slot, part, index):
        ref = wck_region(slot, part, None)
        push(ref, ref, kc_send.at[index], kc_recv.at[index], h.core)

    gather_k = Gather(
        h, wck_region, lambda part: w_ckv.at[pl.ds(c * 512 + part * 128, 128)], k_send, k_recv, share, h.xo
    )
    gather_k.begin_x(0)
    gather_k.begin_x(1)
    steps_k = gather_k.steps()

    others = [(0, 1), (1, 0), (3, 0), (1, 1), (3, 1), (2, 0), (2, 1)]
    for i, (dy, other) in enumerate(others):
        push(w_ckv.at[ck_rows], wck.at[t, ck_rows], p_send.at[0, i], p_recv.at[0, i], h.any_copy(dy, other))
    push(w_eq.at[halves], enc_w.at[0, s, c], x_send.at[1], x_recv.at[1], h.x2)
    push(w_eo.at[halves], enc_w.at[1, s, c], x_send.at[2], x_recv.at[2], h.x2)
    for i, (dy, other) in enumerate(others):
        cols = pl.ds(pl.multiple_of(h.slot(dy, other) * 512, 512), 512)
        push(
            w_co.at[co_rows, cols], woc.at[t, z * 2 + c], p_send.at[1, i], p_recv.at[1, i],
            h.any_copy(dy, other),
        )

    own_hid.wait()
    own_skv.wait()
    own_cq.wait()
    project(t, 0, None)
    project(t, 1, None)

    def both(steps, n=1):
        for _ in range(n):
            for one in steps:
                advance(one)

    both(steps_h, 2)
    both(steps_t)
    both(steps_h, 3)
    both(steps_t)
    own_eq.wait()
    own_eo.wait()
    advance(steps_e[0])
    both(steps_h, 3)
    both(steps_t)
    for w in range(2):
        came(enc_w.at[w, z * 2 + 1 - xh, c], x_recv.at[1 + w])
    advance(steps_e[1])
    both(steps_h, 2)
    both(steps_t)

    for r in rings_t:
        r.collect()

    def pick(owner):
        for k in range(4):
            at = p * 8 + owner - offsets[owner, k]
            at = jnp.minimum(jnp.maximum(at, 0), 254)
            picked[owner, 128 * k : 128 * k + 64, :] = tr[at]
            picked[owner, 128 * k + 64 : 128 * k + 128, :] = tr[at + 1]

    columns = pl.ds(pl.multiple_of(t * 128, 128), 128)
    for i in range(1, TP):
        to = h.tp_peer(i)
        pick(to)
        push(picked.at[to], rows.at[:, columns], p_send.at[3, i], p_recv.at[3, i], h.at_tp(to))
    pick(t)
    rows[:, columns] = picked[t]

    both(steps_h, 2)
    both(steps_e)
    both(steps_h, 2)

    inverse = lax.rsqrt(ssq[...] * (1.0 / 4096) + EPS)
    projected = (acc[...] * inverse).astype(BF)
    kv_s[...] = projected[:, :256]
    q_s[0:512, :] = projected[:, 256:]
    q_s[512:576, :] = jnp.zeros((64, 256), BF)
    for i in range(1, TP):
        to = h.tp_peer(i)
        mine_there = pl.ds(pl.multiple_of(to * 64, 64), 64)
        push(kv_s.at[mine_there], kvx.at[t], p_send.at[2, i], p_recv.at[2, i], h.at_tp(to))
    kvx[t] = kv_s[pl.ds(pl.multiple_of(t * 64, 64), 64), :]

    for i in range(1, TP):
        to = h.tp_peer(i)
        mine_there = pl.ds(pl.multiple_of(to * 64 + 48, 16), 80)
        push(q_s.at[mine_there], qx.at[t], p_send.at[4, i], p_recv.at[4, i], h.at_tp(to))
    qx[t] = q_s[pl.ds(pl.multiple_of(t * 64 + 48, 16), 80), :]
    push(q_s.at[pl.ds(0, 64)], qh.at[t], halo_send.at[0], halo_recv.at[t], h.last_before())

    both(steps_e)
    for copy in own_ckv:
        copy.wait()
    for i, (dy, other) in enumerate(others):
        came(wck.at[h.slot(4 - dy, other), ck_rows], p_recv.at[0, i])
    both(steps_e)
    both(steps_k2)
    own_co.wait()
    for i, (dy, other) in enumerate(others):
        came(woc.at[h.slot(4 - dy, other), z * 2 + c], p_recv.at[1, i])

    def from_peer(i):
        return h.tp_peer(TP - i)

    for i in range(1, TP):
        cols = pl.ds(pl.multiple_of(from_peer(i) * 128, 128), 128)
        came(rows.at[:, cols], p_recv.at[3, i])
    gather_k.begin_y(1)
    gather_k.begin_y(0)
    advance(steps_k, 1)
    both(steps_e)
    both(steps_k2)
    for r in rings_e:
        r.collect()
    for n in range(4):
        cols = slice(256 * n, 256 * (n + 1))
        eq[:, cols] = dot(rows[...], enc_w[0, :, :, :, cols].reshape(1024, 256)).astype(BF)
    advance(steps_k, 2)
    both(steps_k2)
    for i in range(1, TP):
        came(kvx.at[from_peer(i)], p_recv.at[2, i])
    advance(steps_k, 2)
    for e in range(8):
        cols = slice(128 * e, 128 * (e + 1))
        scores = dot_t(eq[:, cols], kvx[e, :, :128]) * FACTOR
        top = jnp.max(scores, axis=-1, keepdims=True)
        weights = jnp.exp(scores - top)
        probs = (weights / jnp.sum(weights, axis=-1, keepdims=True)).astype(BF)
        ea[:, cols] = dot(probs, kvx[e, :, 128:]).astype(BF)
        advance(steps_k, 1)
        if e == 3:
            both(steps_k2)
            both(steps_o)
    for n in range(4):
        cols = slice(256 * n, 256 * (n + 1))
        update = dot(ea[...], enc_w[1, :, :, :, cols].reshape(1024, 256))
        enc[:, cols] = (rows[:, cols].astype(F32) + update).astype(BF)
        advance(steps_k, 1)
    both(steps_k2)
    both(steps_o)

    for i in range(1, TP):
        came(qx.at[from_peer(i)], p_recv.at[4, i])

    @pl.when(is_last)
    def _():
        for j in range(TP):
            came(qh.at[j], halo_recv.at[j])
            qx[j, 16:80, :] = qh[j]

    for index, (slot, part) in enumerate(gather_k.order()):
        came(wck.at[slot, pl.ds((1 - c) * 512 + part * 128, 128)], kc_recv.at[index])
    for r in rings_k:
        r.collect()

    live_keys = counts[t] * 128
    lane = lax.broadcasted_iota(jnp.int32, (80, 512), 1)
    mask = lane < live_keys
    row = lax.broadcasted_iota(jnp.int32, (80, 128), 0)
    keep = (row >= 15) & (row < 79)

    def att_gather(i):
        def region(slot, part, half):
            base = i * 1024 + part * 512
            if half is None:
                return attg.at[slot, :, pl.ds(base, 512)]
            return attg.at[slot, :, pl.ds(base + half * 256, 256)]

        def own(part):
            return att_own.at[:, pl.ds(i * 1024 + part * 512, 512)]

        return Gather(h, region, own, a_send.at[i], a_recv.at[i], lambda *_: None, h.xp)

    gather_a = [att_gather(0), att_gather(1)]
    steps_a = [g.steps() for g in gather_a]

    def tail_copy(j):
        return remote(
            att_own.at[pl.ds(16, 64), pl.ds(256 * j, 256)], tail.at[j],
            tail_send.at[j], tail_recv.at[0], h.at_after(j),
        )

    for j in range(TP):
        pair = dot(enc[...], wck[j]).astype(BF)
        for half in range(2):
            key = pair[:, 256 * half : 256 * half + 128]
            value = pair[:, 256 * half + 128 : 256 * half + 256]
            query = qx[j, :, 128 * half : 128 * half + 128]
            scores = jnp.where(mask, dot_t(query, key) * FACTOR, NEG)
            top = jnp.max(scores, axis=-1, keepdims=True)
            weights = jnp.where(mask, jnp.exp(scores - top), 0.0)
            total = jnp.sum(weights, axis=-1, keepdims=True)
            total = jnp.where(total > 0.0, total, 1.0)
            probs = (weights / total).astype(BF)
            mixed = jnp.where(keep, dot(probs, value), 0.0).astype(BF)
            at = 256 * j + 128 * half
            att_own[:, at : at + 128] = mixed

        @pl.when(is_last)
        def _():
            tail_copy(j).start()

        if j == 1:
            gather_a[0].begin(0)
        if j == 3:
            gather_a[0].begin(1)
            both(steps_o)
        if j == 4:
            advance(steps_a[0], 1)
        if j == 5:
            gather_a[1].begin(0)
            both(steps_o)
        if j == 6:
            advance(steps_a[0], 3)
    gather_a[1].begin(1)
    both(steps_o)
    advance(steps_a[0], 2)
    came(tail.at[t], tail_recv.at[0])
    for i in range(1, TP):
        push(tail.at[t], tail.at[t], p_send.at[5, i], p_recv.at[5, i], h.at_tp(h.tp_peer(i)))
    advance(steps_a[0], 1)
    advance(steps_a[1], 2)
    advance(steps_a[0], 2)
    advance(steps_a[1], 2)
    advance(steps_a[0], 3)
    advance(steps_a[1], 3)
    advance(steps_a[0], 2)
    attg[t] = att_own[...]
    for i in range(1, TP):
        came(tail.at[from_peer(i)], p_recv.at[5, i])
    for r in rings_o:
        r.collect()

    def attended(i):
        cols = slice(1024 * i, 1024 * (i + 1))
        for j in range(4 * i, 4 * i + 4):
            attb[0:64, 256 * j : 256 * (j + 1)] = jnp.where(p > 0, tail[j].astype(F32), 0.0).astype(BF)
        for v in range(TP):
            if v:
                attb[64 * v : 64 * v + 64, cols] = attg[v - 1, 16:80, cols]
            attb[64 * v + 48 : 64 * v + 64, cols] += attg[v, 0:16, cols]
        return dot(attb[:, cols], woc[4 * i : 4 * i + 4].reshape(1024, 512))

    acc[...] = hid[t].astype(F32) + attended(0)
    advance(steps_a[1], 7)
    out[...] = (acc[...] + attended(1)).astype(BF)

    for group in gather_h + [gather_k] + gather_a + rings:
        group.finish()
    for copy in pushes:
        copy.wait_send()

    @pl.when(is_last)
    def _():
        for j in range(TP):
            tail_copy(j).wait_send()


def body(hidden, gain, trace, counts, offsets, w_skv, w_eq, w_eo, w_cq, w_ckv, w_co):
    any_ = pl.BlockSpec(memory_space=pl.ANY)
    vmem = pl.BlockSpec(memory_space=pltpu.VMEM)
    smem = pl.BlockSpec(memory_space=pltpu.SMEM)
    dma = pltpu.SemaphoreType.DMA
    v = pltpu.VMEM
    scratch = [
        v((8, 512, 512), BF),
        v((4096, 512), BF),
        v((512, 512), F32),
        v((512, 1), F32),
        v((512, 256), BF),
        v((576, 256), BF),
        v((256, 64, 128), BF),
        v((8, 512, 128), BF),
        v((512, 1024), BF),
        v((2, 16, 2, 32, 1024), BF),
        v((8, 1024, 512), BF),
        v((8, 16, 16, 512), BF),
        v((8, 64, 256), BF),
        v((8, 80, 256), BF),
        v((8, 64, 256), BF),
        v((512, 1024), BF),
        v((512, 1024), BF),
        v((512, 1024), BF),
        v((80, 2048), BF),
        v((8, 80, 2048), BF),
        v((8, 64, 256), BF),
        v((512, 2048), BF),
        dma((10,)),
        dma((2, 18)), dma((2, 18)), dma((18,)), dma((18,)), dma((2, 18)), dma((2, 18)), dma((14,)), dma((14,)),
        dma((3,)), dma((3,)),
        dma((8, 8)), dma((8, 8)), dma((8, 8)), dma((8, 8)),
        dma((6, 8)), dma((6, 8)),
        dma((1,)), dma((8,)), dma((8,)), dma((1,)),
    ]
    return pl.pallas_call(
        kernel,
        out_shape=jax.ShapeDtypeStruct((512, 512), BF),
        in_specs=[any_, vmem, any_, smem, smem, any_, any_, any_, any_, any_, any_],
        out_specs=vmem,
        scratch_shapes=scratch,
        compiler_params=pltpu.CompilerParams(
            collective_id=0, has_side_effects=True, vmem_limit_bytes=58 << 20
        ),
        cost_estimate=pl.CostEstimate(flops=11_000_000_000, bytes_accessed=14_000_000, transcendentals=1_000_000),
    )(
        hidden, gain.astype(F32).reshape(8, 1, 512), trace.reshape(8, 64, 128), counts, offsets,
        w_skv, w_eq, w_eo, w_cq, w_ckv, w_co,
    )


def solution(mesh):
    place = ("seq", "section")
    in_specs = (
        P(place, "tp"), P(), P(place, "tp"), P(place), P(place, None), P(None, "tp"),
        P("section", None), P("section", None), P(None, "tp"), P(None, "tp"), P("tp", None),
    )
    return jax.shard_map(body, mesh=mesh, in_specs=in_specs, out_specs=P(place, "tp"), check_vma=False)
```

```python
import functools
import math

import jax
import jax.numpy as jnp
from jax import lax
from jax.experimental import pallas as pl
from jax.experimental.pallas import tpu as pltpu
from jax.sharding import PartitionSpec as P

MESH = pl.DeviceIdType.MESH
BF = jnp.bfloat16
F32 = jnp.float32
EPS = 1e-05
NEG = -1e30
FACTOR = 1.0 / math.sqrt(128)
TP = 8
PLACES = 32


def remote(src, dst, send, recv, to):
    return pltpu.make_async_remote_copy(
        src_ref=src, dst_ref=dst, send_sem=send, recv_sem=recv, device_id=to, device_id_type=MESH
    )


def dot(a, b):
    return jnp.dot(a, b, preferred_element_type=F32)


def dot_t(a, b):
    return lax.dot_general(a, b, (((1,), (1,)), ((), ())), preferred_element_type=F32)


class Here:
    def __init__(self):
        self.c = lax.axis_index("seq")
        self.t = lax.axis_index("tp")
        self.s = lax.axis_index("section")
        self.y, self.xl = self.t // 2, self.t % 2
        self.z, self.xh = self.s // 2, self.s % 2
        self.p = self.c * 16 + self.s
        c, t, s = self.c, self.t, self.s
        self.yp = (c, self.slot(1, 0), s)
        self.ym = (c, self.slot(3, 0), s)
        self.xp = (c, self.slot(0, 1), s)
        self.zp = (c, t, ((self.z + 1) % 8) * 2 + self.xh)
        self.zm = (c, t, ((self.z + 7) % 8) * 2 + self.xh)
        self.x2 = (c, t, self.z * 2 + 1 - self.xh)
        self.xo = (c, self.slot(0, 1), self.z * 2 + 1 - self.xh)
        self.core = (1 - c, t, s)
        before, after = (self.p + PLACES - 1) % PLACES, (self.p + 1) % PLACES
        self.before = (before // 16, before % 16)
        self.after = (after // 16, after % 16)

    def slot(self, dy, other):
        xl = 1 - self.xl if other else self.xl
        return ((self.y + dy) % 4) * 2 + xl

    def tp_peer(self, i):
        return (self.t + i) % TP

    def any_copy(self, dy, other):
        return (self.c, self.slot(dy, other), self.z * 2 + (1 - self.xh if other else self.xh))

    def at_tp(self, t):
        return (self.c, t, self.s)

    def last_before(self):
        return (self.before[0], TP - 1, self.before[1])

    def at_after(self, t):
        return (self.after[0], t, self.after[1])


class Gather:
    def __init__(self, here, region, own, send, recv, arrived, xp):
        self.here, self.region, self.own, self.xp = here, region, own, xp
        self.send_sem, self.recv_sem, self.arrived = send, recv, arrived
        self.sent = []

    def send(self, m, to, slot, part, half=None, own=False):
        src = self.own(part) if own else self.region(slot, part, half)
        copy = remote(src, self.region(slot, part, half), self.send_sem.at[m], self.recv_sem.at[m], to)
        copy.start()
        self.sent.append(copy)

    def wait(self, m, slot, part, half=None):
        ref = self.region(slot, part, half)
        remote(ref, ref, self.send_sem.at[m], self.recv_sem.at[m], self.xp).wait_recv()

    def begin(self, part):
        if part == 0:
            self.begin_x(0)
            self.begin_y(0)
        else:
            self.begin_y(1)
            self.begin_x(1)

    def begin_x(self, part):
        self.send(3 * part, self.xp, self.here.t, part, own=True)

    def begin_y(self, part):
        h = self.here
        self.send(3 * part + 1, h.yp, h.t, part, own=True)
        self.send(3 * part + 2, h.ym, h.t, part, own=True)

    def steps(self):
        h = self.here
        slot = h.slot
        self.wait(0, slot(0, 1), 0)
        self.send(6, h.yp, slot(0, 1), 0)
        self.send(7, h.ym, slot(0, 1), 0)
        self.arrived(slot(0, 1), 0, 0)
        yield
        self.wait(4, slot(3, 0), 1)
        self.send(12, self.xp, slot(3, 0), 1)
        self.send(14, h.yp, slot(3, 0), 1, 0)
        self.arrived(slot(3, 0), 1, 1)
        yield
        self.wait(5, slot(1, 0), 1)
        self.send(13, self.xp, slot(1, 0), 1)
        self.send(15, h.ym, slot(1, 0), 1, 1)
        self.arrived(slot(1, 0), 1, 2)
        yield
        self.wait(1, slot(3, 0), 0)
        self.send(8, h.yp, slot(3, 0), 0, 0)
        self.arrived(slot(3, 0), 0, 3)
        yield
        self.wait(2, slot(1, 0), 0)
        self.send(9, h.ym, slot(1, 0), 0, 1)
        self.arrived(slot(1, 0), 0, 4)
        yield
        self.wait(3, slot(0, 1), 1)
        self.arrived(slot(0, 1), 1, 5)
        yield
        self.wait(14, slot(2, 0), 1, 0)
        self.send(16, self.xp, slot(2, 0), 1, 0)
        self.wait(15, slot(2, 0), 1, 1)
        self.send(17, self.xp, slot(2, 0), 1, 1)
        self.arrived(slot(2, 0), 1, 6)
        yield
        self.wait(6, slot(3, 1), 0)
        self.send(10, h.yp, slot(3, 1), 0, 0)
        self.arrived(slot(3, 1), 0, 7)
        yield
        self.wait(7, slot(1, 1), 0)
        self.send(11, h.ym, slot(1, 1), 0, 1)
        self.arrived(slot(1, 1), 0, 8)
        yield
        self.wait(8, slot(2, 0), 0, 0)
        self.wait(9, slot(2, 0), 0, 1)
        self.arrived(slot(2, 0), 0, 9)
        yield
        self.wait(12, slot(3, 1), 1)
        self.arrived(slot(3, 1), 1, 10)
        yield
        self.wait(13, slot(1, 1), 1)
        self.arrived(slot(1, 1), 1, 11)
        yield
        self.wait(10, slot(2, 1), 0, 0)
        self.wait(11, slot(2, 1), 0, 1)
        self.arrived(slot(2, 1), 0, 12)
        yield
        self.wait(16, slot(2, 1), 1, 0)
        self.wait(17, slot(2, 1), 1, 1)
        self.arrived(slot(2, 1), 1, 13)

    def order(self):
        s = self.here.slot
        return [
            (s(0, 1), 0), (s(3, 0), 1), (s(1, 0), 1), (s(3, 0), 0), (s(1, 0), 0), (s(0, 1), 1), (s(2, 0), 1),
            (s(3, 1), 0), (s(1, 1), 0), (s(2, 0), 0), (s(3, 1), 1), (s(1, 1), 1), (s(2, 1), 0), (s(2, 1), 1),
        ]

    def finish(self):
        for copy in self.sent:
            copy.wait_send()


class Ring:
    OFFSET = [0, 7, 1, 6, 2, 5, 3, 4]

    def __init__(self, here, region, sems, flip):
        self.here, self.region, self.flip = here, region, flip
        self.send_sem, self.recv_sem, self.core_send, self.core_recv = sems
        self.sent = []

    def push(self, way, r):
        h = self.here
        z = (h.z + (8 - r if way == 0 else r)) % 8
        ref = self.region(z, h.c)
        m = way * 4 + r
        copy = remote(ref, ref, self.send_sem.at[m], self.recv_sem.at[m], h.zp if way == 0 else h.zm)
        copy.start()
        self.sent.append(copy)

    def share(self, k):
        h = self.here
        ref = self.region((h.z + self.dz(k)) % 8, h.c)
        copy = remote(ref, ref, self.core_send.at[k], self.core_recv.at[k], h.core)
        copy.start()
        self.sent.append(copy)

    def dz(self, k):
        return self.OFFSET[k] if not self.flip else (8 - self.OFFSET[k]) % 8

    def wait(self, way, r, k):
        h = self.here
        ref = self.region((h.z + self.dz(k)) % 8, h.c)
        m = way * 4 + r
        remote(ref, ref, self.send_sem.at[m], self.recv_sem.at[m], h.zp).wait_recv()

    def steps(self):
        first, second = (1, 0) if self.flip else (0, 1)
        self.push(first, 0)
        self.push(second, 0)
        self.share(0)
        yield
        for r in range(3):
            self.wait(first, r, 1 + 2 * r)
            self.push(first, r + 1)
            self.share(1 + 2 * r)
            self.wait(second, r, 2 + 2 * r)
            if r < 2:
                self.push(second, r + 1)
            self.share(2 + 2 * r)
            yield
        self.wait(first, 3, 7)
        self.share(7)
        yield

    def collect(self):
        h = self.here
        for k in range(8):
            ref = self.region((h.z + self.dz(k)) % 8, 1 - h.c)
            remote(ref, ref, self.core_send.at[k], self.core_recv.at[k], h.core).wait_recv()

    def finish(self):
        for copy in self.sent:
            copy.wait_send()


def advance(steps, n=1):
    for _ in range(n):
        next(steps, None)


def kernel(
    hidden, gain_in, trace, counts, offsets, w_skv, w_eq, w_eo, w_cq, w_ckv, w_co, out,
    gain, hid, wproj, acc, ssq, kv_s, q_s, tr, picked, rows, enc_w, wck, woc, kvx, qx, qh, eq, ea, enc,
    att_own, attg, tail, attb,
    local, h_send, h_recv, k_send, k_recv, a_send, a_recv, kc_send, kc_recv,
    x_send, x_recv, r_ss, r_rs, r_cs, r_cr,
    p_send, p_recv, halo_send, halo_recv, tail_send, tail_recv,
):
    h = Here()
    c, t, s, z, xh, p = h.c, h.t, h.s, h.z, h.xh, h.p
    is_last = t == TP - 1

    barrier = pltpu.get_barrier_semaphore()
    greet = [h.at_tp(h.tp_peer(i)) for i in range(1, TP)]
    greet += [h.any_copy(dy, 1) for dy in range(4)]
    greet += [h.zp, h.zm, h.x2, h.core, h.last_before()]
    for device in greet:
        pl.semaphore_signal(barrier, inc=1, device_id=device, device_id_type=MESH)

    @pl.when(is_last)
    def _():
        for other in range(TP):
            pl.semaphore_signal(barrier, inc=1, device_id=h.at_after(other), device_id_type=MESH)

    pl.semaphore_wait(barrier, len(greet) + TP * (t // (TP - 1)))

    pushes = []

    def push(src, dst, send, recv, to):
        copy = remote(src, dst, send, recv, to)
        copy.start()
        pushes.append(copy)

    def came(ref, recv):
        remote(ref, ref, p_send.at[0, 0], recv, h.core).wait_recv()

    def bring(src, dst, i):
        copy = pltpu.make_async_copy(src, dst, local.at[i])
        copy.start()
        return copy

    def project(slot, part, index):
        here = pl.ds(part * 256, 256)
        wide = hid[slot, here, :].astype(F32)
        squares = jnp.sum(wide * wide, axis=-1, keepdims=True)
        scaled = (wide * gain[slot]).astype(BF)
        w = wproj[pl.ds(pl.multiple_of(slot * 512, 512), 512), :]
        product = dot(scaled, w)
        if index is None:
            ssq[here, :] = squares
            acc[here, :] = product
        else:
            ssq[here, :] += squares
            acc[here, :] += product

    def hid_gather(i):
        def region(slot, part, half):
            base = part * 256 + i * 128
            if half is None:
                return hid.at[slot, pl.ds(base, 128)]
            return hid.at[slot, pl.ds(base + half * 64, 64)]

        def own(part):
            return hidden.at[pl.ds(part * 256 + i * 128, 128)]

        def arrived(slot, part, index):
            if i == 1:
                project(slot, part, index)

        return Gather(h, region, own, h_send.at[i], h_recv.at[i], arrived, h.xp)

    gather_h = [hid_gather(0), hid_gather(1)]
    for g in gather_h:
        g.begin(0)
        g.begin(1)
    steps_h = [g.steps() for g in gather_h]

    mine = pl.ds(p * 8, 8)
    halves = pl.ds(c * 32, 32)
    push(trace, tr.at[mine], x_send.at[0], x_recv.at[0], h.x2)
    own_trace = bring(trace, tr.at[mine], 0)
    own_hid = bring(hidden, hid.at[t], 1)
    own_skv = bring(w_skv, wproj.at[:, pl.ds(0, 256)], 2)
    own_cq = bring(w_cq, wproj.at[:, pl.ds(256, 256)], 3)
    own_eq = bring(w_eq.at[halves], enc_w.at[0, s, c], 4)
    own_eo = bring(w_eo.at[halves], enc_w.at[1, s, c], 5)
    own_ckv = [bring(w_ckv.at[pl.ds(512 * i, 256)], wck.at[t, pl.ds(512 * i, 256)], 6 + i) for i in range(2)]
    ck_rows = pl.ds(c * 512 + 256 + z * 32, 32)
    own_ckv.append(bring(w_ckv.at[ck_rows], wck.at[t, ck_rows], 8))
    co_rows = pl.ds(z * 32 + c * 16, 16)
    own_co = bring(w_co.at[co_rows, pl.ds(pl.multiple_of(t * 512, 512), 512)], woc.at[t, z * 2 + c], 9)

    def ring(i, region, flip):
        return Ring(h, region, (r_ss.at[i], r_rs.at[i], r_cs.at[i], r_cr.at[i]), flip)

    def trace_ring(i, sel):
        return ring(i, lambda zz, cc: tr.at[pl.ds((cc * 16 + zz * 2 + sel) * 8, 8)], bool(i % 2))

    def enc_ring(i, sel):
        return ring(i, lambda zz, cc: enc_w.at[:, zz * 2 + sel, cc], bool(i % 2))

    def ckv_ring(i):
        return ring(
            i, lambda zz, cc: wck.at[pl.ds(4 * (i % 2), 4), pl.ds(cc * 512 + 256 + zz * 32, 32)], bool(i % 2)
        )

    def co_ring(i):
        return ring(i, lambda zz, cc: woc.at[pl.ds(4 * (i % 2), 4), zz * 2 + cc], bool(i % 2))

    rings_t = [trace_ring(0, xh), trace_ring(1, 1 - xh)]
    rings_e = [enc_ring(2, xh), enc_ring(3, 1 - xh)]
    rings_k = [ckv_ring(4), ckv_ring(5)]
    rings_o = [co_ring(6), co_ring(7)]
    rings = rings_t + rings_e + rings_k + rings_o
    steps_t, steps_e, steps_k2, steps_o = (
        [r.steps() for r in group] for group in (rings_t, rings_e, rings_k, rings_o)
    )

    own_trace.wait()
    advance(steps_t[0])
    came(tr.at[pl.ds((p + 1 - 2 * xh) * 8, 8)], x_recv.at[0])
    advance(steps_t[1])

    def wck_region(slot, part, half):
        base = c * 512 + part * 128
        if half is None:
            return wck.at[slot, pl.ds(base, 128)]
        return wck.at[slot, pl.ds(base + half * 64, 64)]

    def share(slot, part, index):
        ref = wck_region(slot, part, None)
        push(ref, ref, kc_send.at[index], kc_recv.at[index], h.core)

    gather_k = Gather(
        h, wck_region, lambda part: w_ckv.at[pl.ds(c * 512 + part * 128, 128)], k_send, k_recv, share, h.xo
    )
    gather_k.begin_x(0)
    gather_k.begin_x(1)
    steps_k = gather_k.steps()

    others = [(0, 1), (1, 0), (3, 0), (1, 1), (3, 1), (2, 0), (2, 1)]
    for i, (dy, other) in enumerate(others):
        push(w_ckv.at[ck_rows], wck.at[t, ck_rows], p_send.at[0, i], p_recv.at[0, i], h.any_copy(dy, other))
    push(w_eq.at[halves], enc_w.at[0, s, c], x_send.at[1], x_recv.at[1], h.x2)
    push(w_eo.at[halves], enc_w.at[1, s, c], x_send.at[2], x_recv.at[2], h.x2)
    for i, (dy, other) in enumerate(others):
        cols = pl.ds(pl.multiple_of(h.slot(dy, other) * 512, 512), 512)
        push(
            w_co.at[co_rows, cols], woc.at[t, z * 2 + c], p_send.at[1, i], p_recv.at[1, i],
            h.any_copy(dy, other),
        )

    for i in range(TP):
        gain[i] = gain_in[512 * i : 512 * (i + 1)].astype(F32).reshape(1, 512)
    own_hid.wait()
    own_skv.wait()
    own_cq.wait()
    project(t, 0, None)
    project(t, 1, None)

    def both(steps, n=1):
        for _ in range(n):
            for one in steps:
                advance(one)

    both(steps_h, 2)
    both(steps_t)
    both(steps_h, 3)
    both(steps_t)
    own_eq.wait()
    own_eo.wait()
    advance(steps_e[0])
    both(steps_h, 3)
    both(steps_t)
    for w in range(2):
        came(enc_w.at[w, z * 2 + 1 - xh, c], x_recv.at[1 + w])
    advance(steps_e[1])
    both(steps_h, 2)
    both(steps_t)

    for r in rings_t:
        r.collect()

    def pick(owner):
        for k in range(4):
            at = p * 8 + owner - offsets[k, owner]
            at = jnp.minimum(jnp.maximum(at, 0), 254)
            picked[owner, 128 * k : 128 * k + 64, :] = tr[at]
            picked[owner, 128 * k + 64 : 128 * k + 128, :] = tr[at + 1]

    columns = pl.ds(pl.multiple_of(t * 128, 128), 128)
    for i in range(1, TP):
        to = h.tp_peer(i)
        pick(to)
        push(picked.at[to], rows.at[:, columns], p_send.at[3, i], p_recv.at[3, i], h.at_tp(to))
    pick(t)
    rows[:, columns] = picked[t]

    both(steps_h, 2)
    both(steps_e)
    both(steps_h, 2)

    inverse = lax.rsqrt(ssq[...] * (1.0 / 4096) + EPS)
    projected = (acc[...] * inverse).astype(BF)
    kv_s[...] = projected[:, :256]
    q_s[0:512, :] = projected[:, 256:]
    q_s[512:576, :] = jnp.zeros((64, 256), BF)
    for i in range(1, TP):
        to = h.tp_peer(i)
        mine_there = pl.ds(pl.multiple_of(to * 64, 64), 64)
        push(kv_s.at[mine_there], kvx.at[t], p_send.at[2, i], p_recv.at[2, i], h.at_tp(to))
    kvx[t] = kv_s[pl.ds(pl.multiple_of(t * 64, 64), 64), :]

    for i in range(1, TP):
        to = h.tp_peer(i)
        mine_there = pl.ds(pl.multiple_of(to * 64 + 48, 16), 80)
        push(q_s.at[mine_there], qx.at[t], p_send.at[4, i], p_recv.at[4, i], h.at_tp(to))
    qx[t] = q_s[pl.ds(pl.multiple_of(t * 64 + 48, 16), 80), :]
    push(q_s.at[pl.ds(0, 64)], qh.at[t], halo_send.at[0], halo_recv.at[t], h.last_before())

    both(steps_e)
    for copy in own_ckv:
        copy.wait()
    for i, (dy, other) in enumerate(others):
        came(wck.at[h.slot(4 - dy, other), ck_rows], p_recv.at[0, i])
    both(steps_e)
    both(steps_k2)
    own_co.wait()
    for i, (dy, other) in enumerate(others):
        came(woc.at[h.slot(4 - dy, other), z * 2 + c], p_recv.at[1, i])

    def from_peer(i):
        return h.tp_peer(TP - i)

    for i in range(1, TP):
        cols = pl.ds(pl.multiple_of(from_peer(i) * 128, 128), 128)
        came(rows.at[:, cols], p_recv.at[3, i])
    gather_k.begin_y(1)
    gather_k.begin_y(0)
    advance(steps_k, 1)
    both(steps_e)
    both(steps_k2)
    for r in rings_e:
        r.collect()
    for n in range(4):
        cols = slice(256 * n, 256 * (n + 1))
        eq[:, cols] = dot(rows[...], enc_w[0, :, :, :, cols].reshape(1024, 256)).astype(BF)
    advance(steps_k, 2)
    both(steps_k2)
    for i in range(1, TP):
        came(kvx.at[from_peer(i)], p_recv.at[2, i])
    advance(steps_k, 2)
    for e in range(8):
        cols = slice(128 * e, 128 * (e + 1))
        scores = dot_t(eq[:, cols], kvx[e, :, :128]) * FACTOR
        top = jnp.max(scores, axis=-1, keepdims=True)
        weights = jnp.exp(scores - top)
        probs = (weights * (1.0 / jnp.sum(weights, axis=-1, keepdims=True))).astype(BF)
        ea[:, cols] = dot(probs, kvx[e, :, 128:]).astype(BF)
        advance(steps_k, 1)
        if e == 3:
            both(steps_k2)
            both(steps_o)
    for n in range(4):
        cols = slice(256 * n, 256 * (n + 1))
        update = dot(ea[...], enc_w[1, :, :, :, cols].reshape(1024, 256))
        enc[:, cols] = (rows[:, cols].astype(F32) + update).astype(BF)
        advance(steps_k, 1)
    both(steps_k2)
    both(steps_o)

    for i in range(1, TP):
        came(qx.at[from_peer(i)], p_recv.at[4, i])

    @pl.when(is_last)
    def _():
        for j in range(TP):
            came(qh.at[j], halo_recv.at[j])
            qx[j, 16:80, :] = qh[j]

    for index, (slot, part) in enumerate(gather_k.order()):
        came(wck.at[slot, pl.ds((1 - c) * 512 + part * 128, 128)], kc_recv.at[index])
    for r in rings_k:
        r.collect()

    live_keys = counts[t] * 128
    mask = lax.broadcasted_iota(jnp.int32, (160, 512), 1) < live_keys
    any_live = jnp.zeros((64, 128), jnp.int32) + live_keys > 0
    last_row = lax.broadcasted_iota(jnp.int32, (64, 128), 0) == 63

    def att_gather(i):
        def region(slot, part, half):
            base = i * 1024 + part * 512
            if half is None:
                return attg.at[slot, :, pl.ds(base, 512)]
            return attg.at[slot, :, pl.ds(base + half * 256, 256)]

        def own(part):
            return att_own.at[:, pl.ds(i * 1024 + part * 512, 512)]

        return Gather(h, region, own, a_send.at[i], a_recv.at[i], lambda *_: None, h.xp)

    gather_a = [att_gather(0), att_gather(1)]
    steps_a = [g.steps() for g in gather_a]

    def tail_copy(j):
        return remote(
            att_own.at[:, pl.ds(256 * j, 256)], tail.at[j],
            tail_send.at[j], tail_recv.at[0], h.at_after(j),
        )

    for j in range(TP):
        pair = dot(enc[...], wck[j]).astype(BF)
        scores = jnp.concatenate(
            [dot_t(qx[j, :, 128 * i : 128 * i + 128], pair[:, 256 * i : 256 * i + 128]) for i in range(2)], axis=0
        )
        scores = jnp.where(mask, scores * FACTOR, NEG)
        weights = jnp.exp(scores - jnp.max(scores, axis=-1, keepdims=True))
        probs = (weights * (1.0 / jnp.sum(weights, axis=-1, keepdims=True))).astype(BF)
        for i in range(2):
            mixed = dot(probs[80 * i : 80 * i + 80], pair[:, 256 * i + 128 : 256 * i + 256])
            mixed = jnp.where(last_row, mixed[15:16], mixed[16:80])
            at = 256 * j + 128 * i
            att_own[:, at : at + 128] = jnp.where(any_live, mixed, 0.0).astype(BF)

        @pl.when(is_last)
        def _():
            tail_copy(j).start()

        if j == 1:
            gather_a[0].begin(0)
        if j == 3:
            gather_a[0].begin(1)
            both(steps_o)
        if j == 4:
            advance(steps_a[0], 1)
        if j == 5:
            gather_a[1].begin(0)
            both(steps_o)
        if j == 6:
            advance(steps_a[0], 3)
    gather_a[1].begin(1)
    both(steps_o)
    advance(steps_a[0], 2)
    came(tail.at[t], tail_recv.at[0])
    for i in range(1, TP):
        push(tail.at[t], tail.at[t], p_send.at[5, i], p_recv.at[5, i], h.at_tp(h.tp_peer(i)))
    advance(steps_a[0], 1)
    advance(steps_a[1], 2)
    advance(steps_a[0], 2)
    advance(steps_a[1], 2)
    advance(steps_a[0], 3)
    advance(steps_a[1], 3)
    advance(steps_a[0], 2)
    attg[t] = att_own[...]
    for i in range(1, TP):
        came(tail.at[from_peer(i)], p_recv.at[5, i])
    for r in rings_o:
        r.collect()

    own_row = lax.broadcasted_iota(jnp.int32, (16, 1024), 0) == 15

    def attended(i):
        cols = slice(1024 * i, 1024 * (i + 1))
        for j in range(4 * i, 4 * i + 4):
            attb[0:64, 256 * j : 256 * (j + 1)] = jnp.where(p > 0, tail[j].astype(F32), 0.0).astype(BF)
        for v in range(TP):
            if v:
                attb[64 * v : 64 * v + 64, cols] = attg[v - 1, :, cols]
            attb[64 * v + 48 : 64 * v + 64, cols] = jnp.where(
                own_row, attg[v, 48:64, cols], attb[64 * v + 48 : 64 * v + 64, cols]
            )
        return dot(attb[:, cols], woc[4 * i : 4 * i + 4].reshape(1024, 512))

    acc[...] = hid[t].astype(F32) + attended(0)
    advance(steps_a[1], 7)
    out[...] = (acc[...] + attended(1)).astype(BF)

    for group in gather_h + [gather_k] + gather_a + rings:
        group.finish()
    for copy in pushes:
        copy.wait_send()

    @pl.when(is_last)
    def _():
        for j in range(TP):
            tail_copy(j).wait_send()


def body(hidden, gain, trace, counts, offsets, w_skv, w_eq, w_eo, w_cq, w_ckv, w_co):
    any_ = pl.BlockSpec(memory_space=pl.ANY)
    vmem = pl.BlockSpec(memory_space=pltpu.VMEM)
    smem = pl.BlockSpec(memory_space=pltpu.SMEM)
    dma = pltpu.SemaphoreType.DMA
    v = pltpu.VMEM
    scratch = [
        v((8, 1, 512), F32),
        v((8, 512, 512), BF),
        v((4096, 512), BF),
        v((512, 512), F32),
        v((512, 1), F32),
        v((512, 256), BF),
        v((576, 256), BF),
        v((256, 64, 128), BF),
        v((8, 512, 128), BF),
        v((512, 1024), BF),
        v((2, 16, 2, 32, 1024), BF),
        v((8, 1024, 512), BF),
        v((8, 16, 16, 512), BF),
        v((8, 64, 256), BF),
        v((8, 80, 256), BF),
        v((8, 64, 256), BF),
        v((512, 1024), BF),
        v((512, 1024), BF),
        v((512, 1024), BF),
        v((64, 2048), BF),
        v((8, 64, 2048), BF),
        v((8, 64, 256), BF),
        v((512, 2048), BF),
        dma((10,)),
        dma((2, 18)), dma((2, 18)), dma((18,)), dma((18,)), dma((2, 18)), dma((2, 18)), dma((14,)), dma((14,)),
        dma((3,)), dma((3,)),
        dma((8, 8)), dma((8, 8)), dma((8, 8)), dma((8, 8)),
        dma((6, 8)), dma((6, 8)),
        dma((1,)), dma((8,)), dma((8,)), dma((1,)),
    ]
    return pl.pallas_call(
        kernel,
        out_shape=jax.ShapeDtypeStruct((512, 512), BF),
        in_specs=[any_, vmem, any_, smem, smem, any_, any_, any_, any_, any_, any_],
        out_specs=vmem,
        scratch_shapes=scratch,
        compiler_params=pltpu.CompilerParams(
            collective_id=0, has_side_effects=True, vmem_limit_bytes=58 << 20
        ),
        cost_estimate=pl.CostEstimate(flops=11_000_000_000, bytes_accessed=14_000_000, transcendentals=1_000_000),
    )(
        hidden, gain, trace.reshape(8, 64, 128), counts, offsets.T,
        w_skv, w_eq, w_eo, w_cq, w_ckv, w_co,
    )


def solution(mesh):
    place = ("seq", "section")
    in_specs = (
        P(place, "tp"), P(), P(place, "tp"), P(place), P(place, None), P(None, "tp"),
        P("section", None), P("section", None), P(None, "tp"), P(None, "tp"), P("tp", None),
    )
    return jax.shard_map(body, mesh=mesh, in_specs=in_specs, out_specs=P(place, "tp"), check_vma=False)
```

```python
import functools
import math

import jax
import jax.numpy as jnp
from jax import lax
from jax.experimental import pallas as pl
from jax.experimental.pallas import tpu as pltpu
from jax.sharding import PartitionSpec as P

MESH = pl.DeviceIdType.MESH
BF = jnp.bfloat16
F32 = jnp.float32
EPS = 1e-05
NEG = -1e30
FACTOR = 1.0 / math.sqrt(128)
TP = 8
PLACES = 32


def remote(src, dst, send, recv, to):
    return pltpu.make_async_remote_copy(
        src_ref=src, dst_ref=dst, send_sem=send, recv_sem=recv, device_id=to, device_id_type=MESH
    )


def dot(a, b):
    return jnp.dot(a, b, preferred_element_type=F32)


def dot_t(a, b):
    return lax.dot_general(a, b, (((1,), (1,)), ((), ())), preferred_element_type=F32)


class Here:
    def __init__(self):
        self.c = lax.axis_index("seq")
        self.t = lax.axis_index("tp")
        self.s = lax.axis_index("section")
        self.y, self.xl = self.t // 2, self.t % 2
        self.z, self.xh = self.s // 2, self.s % 2
        self.p = self.c * 16 + self.s
        c, t, s = self.c, self.t, self.s
        self.yp = (c, self.slot(1, 0), s)
        self.ym = (c, self.slot(3, 0), s)
        self.xp = (c, self.slot(0, 1), s)
        self.zp = (c, t, ((self.z + 1) % 8) * 2 + self.xh)
        self.zm = (c, t, ((self.z + 7) % 8) * 2 + self.xh)
        self.x2 = (c, t, self.z * 2 + 1 - self.xh)
        self.xo = (c, self.slot(0, 1), self.z * 2 + 1 - self.xh)
        self.core = (1 - c, t, s)
        before, after = (self.p + PLACES - 1) % PLACES, (self.p + 1) % PLACES
        self.before = (before // 16, before % 16)
        self.after = (after // 16, after % 16)

    def slot(self, dy, other):
        xl = 1 - self.xl if other else self.xl
        return ((self.y + dy) % 4) * 2 + xl

    def tp_peer(self, i):
        return (self.t + i) % TP

    def any_copy(self, dy, other):
        return (self.c, self.slot(dy, other), self.z * 2 + (1 - self.xh if other else self.xh))

    def at_tp(self, t):
        return (self.c, t, self.s)

    def last_before(self):
        return (self.before[0], TP - 1, self.before[1])

    def at_after(self, t):
        return (self.after[0], t, self.after[1])


class Gather:
    def __init__(self, here, region, own, send, recv, arrived, xp):
        self.here, self.region, self.own, self.xp = here, region, own, xp
        self.send_sem, self.recv_sem, self.arrived = send, recv, arrived
        self.sent = []

    def send(self, m, to, slot, part, half=None, own=False):
        src = self.own(part) if own else self.region(slot, part, half)
        copy = remote(src, self.region(slot, part, half), self.send_sem.at[m], self.recv_sem.at[m], to)
        copy.start()
        self.sent.append(copy)

    def wait(self, m, slot, part, half=None):
        ref = self.region(slot, part, half)
        remote(ref, ref, self.send_sem.at[m], self.recv_sem.at[m], self.xp).wait_recv()

    def begin(self, part):
        if part == 0:
            self.begin_x(0)
            self.begin_y(0)
        else:
            self.begin_y(1)
            self.begin_x(1)

    def begin_x(self, part):
        self.send(3 * part, self.xp, self.here.t, part, own=True)

    def begin_y(self, part):
        h = self.here
        self.send(3 * part + 1, h.yp, h.t, part, own=True)
        self.send(3 * part + 2, h.ym, h.t, part, own=True)

    def steps(self):
        h = self.here
        slot = h.slot
        self.wait(0, slot(0, 1), 0)
        self.send(6, h.yp, slot(0, 1), 0)
        self.send(7, h.ym, slot(0, 1), 0)
        self.arrived(slot(0, 1), 0, 0)
        yield
        self.wait(4, slot(3, 0), 1)
        self.send(12, self.xp, slot(3, 0), 1)
        self.send(14, h.yp, slot(3, 0), 1, 0)
        self.arrived(slot(3, 0), 1, 1)
        yield
        self.wait(5, slot(1, 0), 1)
        self.send(13, self.xp, slot(1, 0), 1)
        self.send(15, h.ym, slot(1, 0), 1, 1)
        self.arrived(slot(1, 0), 1, 2)
        yield
        self.wait(1, slot(3, 0), 0)
        self.send(8, h.yp, slot(3, 0), 0, 0)
        self.arrived(slot(3, 0), 0, 3)
        yield
        self.wait(2, slot(1, 0), 0)
        self.send(9, h.ym, slot(1, 0), 0, 1)
        self.arrived(slot(1, 0), 0, 4)
        yield
        self.wait(3, slot(0, 1), 1)
        self.arrived(slot(0, 1), 1, 5)
        yield
        self.wait(14, slot(2, 0), 1, 0)
        self.send(16, self.xp, slot(2, 0), 1, 0)
        self.wait(15, slot(2, 0), 1, 1)
        self.send(17, self.xp, slot(2, 0), 1, 1)
        self.arrived(slot(2, 0), 1, 6)
        yield
        self.wait(6, slot(3, 1), 0)
        self.send(10, h.yp, slot(3, 1), 0, 0)
        self.arrived(slot(3, 1), 0, 7)
        yield
        self.wait(7, slot(1, 1), 0)
        self.send(11, h.ym, slot(1, 1), 0, 1)
        self.arrived(slot(1, 1), 0, 8)
        yield
        self.wait(8, slot(2, 0), 0, 0)
        self.wait(9, slot(2, 0), 0, 1)
        self.arrived(slot(2, 0), 0, 9)
        yield
        self.wait(12, slot(3, 1), 1)
        self.arrived(slot(3, 1), 1, 10)
        yield
        self.wait(13, slot(1, 1), 1)
        self.arrived(slot(1, 1), 1, 11)
        yield
        self.wait(10, slot(2, 1), 0, 0)
        self.wait(11, slot(2, 1), 0, 1)
        self.arrived(slot(2, 1), 0, 12)
        yield
        self.wait(16, slot(2, 1), 1, 0)
        self.wait(17, slot(2, 1), 1, 1)
        self.arrived(slot(2, 1), 1, 13)

    def order(self):
        s = self.here.slot
        return [
            (s(0, 1), 0), (s(3, 0), 1), (s(1, 0), 1), (s(3, 0), 0), (s(1, 0), 0), (s(0, 1), 1), (s(2, 0), 1),
            (s(3, 1), 0), (s(1, 1), 0), (s(2, 0), 0), (s(3, 1), 1), (s(1, 1), 1), (s(2, 1), 0), (s(2, 1), 1),
        ]

    def finish(self):
        for copy in self.sent:
            copy.wait_send()


class Ring:
    OFFSET = [0, 7, 1, 6, 2, 5, 3, 4]

    def __init__(self, here, region, sems, flip, cross=None):
        self.here, self.region, self.flip, self.cross = here, region, flip, cross
        self.send_sem, self.recv_sem, self.core_send, self.core_recv = sems
        self.sent = []

    def push(self, way, r):
        h = self.here
        z = (h.z + (8 - r if way == 0 else r)) % 8
        ref = self.region(z, h.c)
        m = way * 4 + r
        copy = remote(ref, ref, self.send_sem.at[m], self.recv_sem.at[m], h.zp if way == 0 else h.zm)
        copy.start()
        self.sent.append(copy)

    def share(self, k):
        h = self.here
        ref = self.region((h.z + self.dz(k)) % 8, h.c)
        copy = remote(ref, ref, self.core_send.at[k], self.core_recv.at[k], h.core)
        copy.start()
        self.sent.append(copy)
        if self.cross:
            copy = remote(ref, ref, self.cross[0].at[k], self.cross[1].at[k], h.xo)
            copy.start()
            self.sent.append(copy)

    def swap(self):
        h = self.here
        for k in range(8):
            ref = self.region((h.z + self.dz(k)) % 8, h.c, 1 - h.xh)
            remote(ref, ref, self.cross[0].at[k], self.cross[1].at[k], h.xo).wait_recv()
            copy = remote(ref, ref, self.cross[2].at[k], self.cross[3].at[k], h.core)
            copy.start()
            self.sent.append(copy)
            yield

    def dz(self, k):
        return self.OFFSET[k] if not self.flip else (8 - self.OFFSET[k]) % 8

    def wait(self, way, r, k):
        h = self.here
        ref = self.region((h.z + self.dz(k)) % 8, h.c)
        m = way * 4 + r
        remote(ref, ref, self.send_sem.at[m], self.recv_sem.at[m], h.zp).wait_recv()

    def steps(self):
        first, second = (1, 0) if self.flip else (0, 1)
        self.push(first, 0)
        self.push(second, 0)
        self.share(0)
        yield
        for r in range(3):
            self.wait(first, r, 1 + 2 * r)
            self.push(first, r + 1)
            self.share(1 + 2 * r)
            self.wait(second, r, 2 + 2 * r)
            if r < 2:
                self.push(second, r + 1)
            self.share(2 + 2 * r)
            yield
        self.wait(first, 3, 7)
        self.share(7)
        yield

    def collect(self):
        h = self.here
        for k in range(8):
            ref = self.region((h.z + self.dz(k)) % 8, 1 - h.c)
            remote(ref, ref, self.core_send.at[k], self.core_recv.at[k], h.core).wait_recv()
            if self.cross:
                ref = self.region((h.z + self.dz(k)) % 8, 1 - h.c, 1 - h.xh)
                remote(ref, ref, self.cross[2].at[k], self.cross[3].at[k], h.core).wait_recv()

    def finish(self):
        for copy in self.sent:
            copy.wait_send()


def advance(steps, n=1):
    for _ in range(n):
        next(steps, None)


def kernel(
    hidden, gain_in, trace, counts, offsets, w_skv, w_eq, w_eo, w_cq, w_ckv, w_co, out,
    gain, hid, wproj, acc, ssq, kv_s, q_s, tr, picked, rows, enc_w, wck, woc, kvx, qx, qh, eq, ea, enc,
    att_own, attg, tail, attb,
    local, h_send, h_recv, k_send, k_recv, a_send, a_recv, kc_send, kc_recv,
    x_send, x_recv, r_ss, r_rs, r_cs, r_cr, s_xs, s_xr, s_cs, s_cr,
    p_send, p_recv, halo_send, halo_recv, tail_send, tail_recv,
):
    h = Here()
    c, t, s, z, xh, p = h.c, h.t, h.s, h.z, h.xh, h.p
    is_last = t == TP - 1

    barrier = pltpu.get_barrier_semaphore()
    greet = [h.at_tp(h.tp_peer(i)) for i in range(1, TP)]
    greet += [h.any_copy(dy, 1) for dy in range(4)]
    greet += [h.zp, h.zm, h.x2, h.core, h.last_before()]
    for device in greet:
        pl.semaphore_signal(barrier, inc=1, device_id=device, device_id_type=MESH)

    @pl.when(is_last)
    def _():
        for other in range(TP):
            pl.semaphore_signal(barrier, inc=1, device_id=h.at_after(other), device_id_type=MESH)

    pl.semaphore_wait(barrier, len(greet) + TP * (t // (TP - 1)))

    pushes = []

    def push(src, dst, send, recv, to):
        copy = remote(src, dst, send, recv, to)
        copy.start()
        pushes.append(copy)

    def came(ref, recv):
        remote(ref, ref, p_send.at[0, 0], recv, h.core).wait_recv()

    def bring(src, dst, i):
        copy = pltpu.make_async_copy(src, dst, local.at[i])
        copy.start()
        return copy

    def project(slot, part, index):
        here = pl.ds(part * 256, 256)
        wide = hid[slot, here, :].astype(F32)
        squares = jnp.sum(wide * wide, axis=-1, keepdims=True)
        scaled = (wide * gain[slot]).astype(BF)
        w = wproj[pl.ds(pl.multiple_of(slot * 512, 512), 512), :]
        product = dot(scaled, w)
        if index is None:
            ssq[here, :] = squares
            acc[here, :] = product
        else:
            ssq[here, :] += squares
            acc[here, :] += product

    def hid_gather(i):
        def region(slot, part, half):
            base = part * 256 + i * 128
            if half is None:
                return hid.at[slot, pl.ds(base, 128)]
            return hid.at[slot, pl.ds(base + half * 64, 64)]

        def own(part):
            return hidden.at[pl.ds(part * 256 + i * 128, 128)]

        def arrived(slot, part, index):
            if i == 1:
                project(slot, part, index)

        return Gather(h, region, own, h_send.at[i], h_recv.at[i], arrived, h.xp)

    gather_h = [hid_gather(0), hid_gather(1)]
    for g in gather_h:
        g.begin(0)
        g.begin(1)
    steps_h = [g.steps() for g in gather_h]

    mine = pl.ds(p * 8, 8)
    halves = pl.ds(c * 32, 32)
    push(trace, tr.at[mine], x_send.at[0], x_recv.at[0], h.x2)
    own_trace = bring(trace, tr.at[mine], 0)
    own_hid = bring(hidden, hid.at[t], 1)
    own_skv = bring(w_skv, wproj.at[:, pl.ds(0, 256)], 2)
    own_cq = bring(w_cq, wproj.at[:, pl.ds(256, 256)], 3)
    own_eq = bring(w_eq.at[halves], enc_w.at[0, s, c], 4)
    own_eo = bring(w_eo.at[halves], enc_w.at[1, s, c], 5)
    own_ckv = [bring(w_ckv.at[pl.ds(512 * i, 256)], wck.at[t, pl.ds(512 * i, 256)], 6 + i) for i in range(2)]
    ck_rows = pl.ds(c * 512 + 256 + z * 32, 32)
    own_ckv.append(bring(w_ckv.at[ck_rows], wck.at[t, ck_rows], 8))
    co_rows = pl.ds(z * 32 + c * 16, 16)
    own_co = bring(w_co.at[co_rows, pl.ds(pl.multiple_of(t * 512, 512), 512)], woc.at[t, z * 2 + c], 9)

    def ring(i, region, flip):
        return Ring(h, region, (r_ss.at[i], r_rs.at[i], r_cs.at[i], r_cr.at[i]), flip)

    def trace_ring(i, sel):
        return ring(i, lambda zz, cc: tr.at[pl.ds((cc * 16 + zz * 2 + sel) * 8, 8)], bool(i % 2))

    def enc_ring(i):
        w = i % 2
        return Ring(
            h, lambda zz, cc, sel=xh: enc_w.at[w, zz * 2 + sel, cc],
            (r_ss.at[i], r_rs.at[i], r_cs.at[i], r_cr.at[i]), bool(w),
            (s_xs.at[w], s_xr.at[w], s_cs.at[w], s_cr.at[w]),
        )

    def ckv_ring(i):
        return ring(
            i, lambda zz, cc: wck.at[pl.ds(4 * (i % 2), 4), pl.ds(cc * 512 + 256 + zz * 32, 32)], bool(i % 2)
        )

    def co_ring(i):
        return ring(i, lambda zz, cc: woc.at[pl.ds(4 * (i % 2), 4), zz * 2 + cc], bool(i % 2))

    rings_t = [trace_ring(0, xh), trace_ring(1, 1 - xh)]
    rings_e = [enc_ring(2), enc_ring(3)]
    rings_k = [ckv_ring(4), ckv_ring(5)]
    rings_o = [co_ring(6), co_ring(7)]
    rings = rings_t + rings_e + rings_k + rings_o
    steps_t, steps_e, steps_k2, steps_o = (
        [r.steps() for r in group] for group in (rings_t, rings_e, rings_k, rings_o)
    )

    own_trace.wait()
    advance(steps_t[0])
    came(tr.at[pl.ds((p + 1 - 2 * xh) * 8, 8)], x_recv.at[0])
    advance(steps_t[1])

    def wck_region(slot, part, half):
        base = c * 512 + part * 128
        if half is None:
            return wck.at[slot, pl.ds(base, 128)]
        return wck.at[slot, pl.ds(base + half * 64, 64)]

    def share(slot, part, index):
        ref = wck_region(slot, part, None)
        push(ref, ref, kc_send.at[index], kc_recv.at[index], h.core)

    gather_k = Gather(
        h, wck_region, lambda part: w_ckv.at[pl.ds(c * 512 + part * 128, 128)], k_send, k_recv, share, h.xo
    )
    gather_k.begin_x(0)
    gather_k.begin_x(1)
    steps_k = gather_k.steps()

    others = [(0, 1), (1, 0), (3, 0), (1, 1), (3, 1), (2, 0), (2, 1)]
    for i, (dy, other) in enumerate(others):
        push(w_ckv.at[ck_rows], wck.at[t, ck_rows], p_send.at[0, i], p_recv.at[0, i], h.any_copy(dy, other))
    for i, (dy, other) in enumerate(others):
        cols = pl.ds(pl.multiple_of(h.slot(dy, other) * 512, 512), 512)
        push(
            w_co.at[co_rows, cols], woc.at[t, z * 2 + c], p_send.at[1, i], p_recv.at[1, i],
            h.any_copy(dy, other),
        )

    for i in range(TP):
        gain[i] = gain_in[512 * i : 512 * (i + 1)].astype(F32).reshape(1, 512)
    own_hid.wait()
    own_skv.wait()
    own_cq.wait()
    project(t, 0, None)
    project(t, 1, None)

    def both(steps, n=1):
        for _ in range(n):
            for one in steps:
                advance(one)

    both(steps_h, 2)
    both(steps_t)
    both(steps_h, 3)
    both(steps_t)
    own_eq.wait()
    own_eo.wait()
    both(steps_e)
    both(steps_h, 3)
    both(steps_t)
    both(steps_e)
    both(steps_h, 2)
    both(steps_t)

    for r in rings_t:
        r.collect()

    def pick(owner):
        for k in range(4):
            at = p * 8 + owner - offsets[k, owner]
            at = jnp.minimum(jnp.maximum(at, 0), 254)
            picked[owner, 128 * k : 128 * k + 64, :] = tr[at]
            picked[owner, 128 * k + 64 : 128 * k + 128, :] = tr[at + 1]

    columns = pl.ds(pl.multiple_of(t * 128, 128), 128)
    for i in range(1, TP):
        to = h.tp_peer(i)
        pick(to)
        push(picked.at[to], rows.at[:, columns], p_send.at[3, i], p_recv.at[3, i], h.at_tp(to))
    pick(t)
    rows[:, columns] = picked[t]

    both(steps_h, 2)
    both(steps_e)
    for copy in own_ckv:
        copy.wait()
    for i, (dy, other) in enumerate(others):
        came(wck.at[h.slot(4 - dy, other), ck_rows], p_recv.at[0, i])
    both(steps_k2)
    both(steps_h, 2)

    inverse = lax.rsqrt(ssq[...] * (1.0 / 4096) + EPS)
    projected = (acc[...] * inverse).astype(BF)
    kv_s[...] = projected[:, :256]
    q_s[0:512, :] = projected[:, 256:]
    q_s[512:576, :] = jnp.zeros((64, 256), BF)
    for i in range(1, TP):
        to = h.tp_peer(i)
        mine_there = pl.ds(pl.multiple_of(to * 64, 64), 64)
        push(kv_s.at[mine_there], kvx.at[t], p_send.at[2, i], p_recv.at[2, i], h.at_tp(to))
    kvx[t] = kv_s[pl.ds(pl.multiple_of(t * 64, 64), 64), :]

    for i in range(1, TP):
        to = h.tp_peer(i)
        mine_there = pl.ds(pl.multiple_of(to * 64 + 48, 16), 80)
        push(q_s.at[mine_there], qx.at[t], p_send.at[4, i], p_recv.at[4, i], h.at_tp(to))
    qx[t] = q_s[pl.ds(pl.multiple_of(t * 64 + 48, 16), 80), :]
    push(q_s.at[pl.ds(0, 64)], qh.at[t], halo_send.at[0], halo_recv.at[t], h.last_before())

    both(steps_e)
    swaps = [r.swap() for r in rings_e]
    both(swaps, 3)
    both(steps_e)
    both(swaps, 2)
    both(steps_k2)
    own_co.wait()
    for i, (dy, other) in enumerate(others):
        came(woc.at[h.slot(4 - dy, other), z * 2 + c], p_recv.at[1, i])

    def from_peer(i):
        return h.tp_peer(TP - i)

    for i in range(1, TP):
        cols = pl.ds(pl.multiple_of(from_peer(i) * 128, 128), 128)
        came(rows.at[:, cols], p_recv.at[3, i])
    gather_k.begin_y(1)
    gather_k.begin_y(0)
    advance(steps_k, 1)
    both(swaps, 3)
    both(steps_k2)
    for r in rings_e:
        r.collect()
    for n in range(4):
        cols = slice(256 * n, 256 * (n + 1))
        eq[:, cols] = dot(rows[...], enc_w[0, :, :, :, cols].reshape(1024, 256)).astype(BF)
    advance(steps_k, 2)
    both(steps_k2)
    for i in range(1, TP):
        came(kvx.at[from_peer(i)], p_recv.at[2, i])
    advance(steps_k, 2)
    for e in range(8):
        cols = slice(128 * e, 128 * (e + 1))
        scores = dot_t(eq[:, cols], kvx[e, :, :128]) * FACTOR
        top = jnp.max(scores, axis=-1, keepdims=True)
        weights = jnp.exp(scores - top)
        probs = (weights * (1.0 / jnp.sum(weights, axis=-1, keepdims=True))).astype(BF)
        ea[:, cols] = dot(probs, kvx[e, :, 128:]).astype(BF)
        advance(steps_k, 1)
        if e == 3:
            both(steps_k2)
            both(steps_o)
    for n in range(4):
        cols = slice(256 * n, 256 * (n + 1))
        update = dot(ea[...], enc_w[1, :, :, :, cols].reshape(1024, 256))
        enc[:, cols] = (rows[:, cols].astype(F32) + update).astype(BF)
        advance(steps_k, 1)
    both(steps_k2)
    both(steps_o)

    for i in range(1, TP):
        came(qx.at[from_peer(i)], p_recv.at[4, i])

    @pl.when(is_last)
    def _():
        for j in range(TP):
            came(qh.at[j], halo_recv.at[j])
            qx[j, 16:80, :] = qh[j]

    for index, (slot, part) in enumerate(gather_k.order()):
        came(wck.at[slot, pl.ds((1 - c) * 512 + part * 128, 128)], kc_recv.at[index])
    for r in rings_k:
        r.collect()

    live_keys = counts[t] * 128
    mask = lax.broadcasted_iota(jnp.int32, (160, 512), 1) < live_keys
    any_live = jnp.zeros((64, 128), jnp.int32) + live_keys > 0
    last_row = lax.broadcasted_iota(jnp.int32, (64, 128), 0) == 63

    def att_gather(i):
        def region(slot, part, half):
            base = i * 1024 + part * 512
            if half is None:
                return attg.at[slot, :, pl.ds(base, 512)]
            return attg.at[slot, :, pl.ds(base + half * 256, 256)]

        def own(part):
            return att_own.at[:, pl.ds(i * 1024 + part * 512, 512)]

        return Gather(h, region, own, a_send.at[i], a_recv.at[i], lambda *_: None, h.xp)

    gather_a = [att_gather(0), att_gather(1)]
    steps_a = [g.steps() for g in gather_a]

    def tail_copy(j):
        return remote(
            att_own.at[:, pl.ds(256 * j, 256)], tail.at[j],
            tail_send.at[j], tail_recv.at[0], h.at_after(j),
        )

    for j in range(TP):
        pair = dot(enc[...], wck[j]).astype(BF)
        scores = jnp.concatenate(
            [dot_t(qx[j, :, 128 * i : 128 * i + 128], pair[:, 256 * i : 256 * i + 128]) for i in range(2)], axis=0
        )
        scores = jnp.where(mask, scores * FACTOR, NEG)
        weights = jnp.exp(scores - jnp.max(scores, axis=-1, keepdims=True))
        probs = (weights * (1.0 / jnp.sum(weights, axis=-1, keepdims=True))).astype(BF)
        for i in range(2):
            mixed = dot(probs[80 * i : 80 * i + 80], pair[:, 256 * i + 128 : 256 * i + 256])
            mixed = jnp.where(last_row, mixed[15:16], mixed[16:80])
            at = 256 * j + 128 * i
            att_own[:, at : at + 128] = jnp.where(any_live, mixed, 0.0).astype(BF)

        @pl.when(is_last)
        def _():
            tail_copy(j).start()

        if j == 1:
            gather_a[0].begin(0)
        if j == 3:
            gather_a[0].begin(1)
            both(steps_o)
        if j == 4:
            advance(steps_a[0], 1)
        if j == 5:
            gather_a[1].begin(0)
            both(steps_o)
        if j == 6:
            advance(steps_a[0], 3)
    gather_a[1].begin(1)
    both(steps_o)
    advance(steps_a[0], 2)
    came(tail.at[t], tail_recv.at[0])
    for i in range(1, TP):
        push(tail.at[t], tail.at[t], p_send.at[5, i], p_recv.at[5, i], h.at_tp(h.tp_peer(i)))
    advance(steps_a[0], 1)
    advance(steps_a[1], 2)
    advance(steps_a[0], 2)
    advance(steps_a[1], 2)
    advance(steps_a[0], 3)
    advance(steps_a[1], 3)
    advance(steps_a[0], 2)
    attg[t] = att_own[...]
    for i in range(1, TP):
        came(tail.at[from_peer(i)], p_recv.at[5, i])
    for r in rings_o:
        r.collect()

    own_row = lax.broadcasted_iota(jnp.int32, (16, 1024), 0) == 15

    def attended(i):
        cols = slice(1024 * i, 1024 * (i + 1))
        for j in range(4 * i, 4 * i + 4):
            attb[0:64, 256 * j : 256 * (j + 1)] = jnp.where(p > 0, tail[j].astype(F32), 0.0).astype(BF)
        for v in range(TP):
            if v:
                attb[64 * v : 64 * v + 64, cols] = attg[v - 1, :, cols]
            attb[64 * v + 48 : 64 * v + 64, cols] = jnp.where(
                own_row, attg[v, 48:64, cols], attb[64 * v + 48 : 64 * v + 64, cols]
            )
        return dot(attb[:, cols], woc[4 * i : 4 * i + 4].reshape(1024, 512))

    acc[...] = hid[t].astype(F32) + attended(0)
    advance(steps_a[1], 7)
    out[...] = (acc[...] + attended(1)).astype(BF)

    for group in gather_h + [gather_k] + gather_a + rings:
        group.finish()
    for copy in pushes:
        copy.wait_send()

    @pl.when(is_last)
    def _():
        for j in range(TP):
            tail_copy(j).wait_send()


def body(hidden, gain, trace, counts, offsets, w_skv, w_eq, w_eo, w_cq, w_ckv, w_co):
    any_ = pl.BlockSpec(memory_space=pl.ANY)
    vmem = pl.BlockSpec(memory_space=pltpu.VMEM)
    smem = pl.BlockSpec(memory_space=pltpu.SMEM)
    dma = pltpu.SemaphoreType.DMA
    v = pltpu.VMEM
    scratch = [
        v((8, 1, 512), F32),
        v((8, 512, 512), BF),
        v((4096, 512), BF),
        v((512, 512), F32),
        v((512, 1), F32),
        v((512, 256), BF),
        v((576, 256), BF),
        v((256, 64, 128), BF),
        v((8, 512, 128), BF),
        v((512, 1024), BF),
        v((2, 16, 2, 32, 1024), BF),
        v((8, 1024, 512), BF),
        v((8, 16, 16, 512), BF),
        v((8, 64, 256), BF),
        v((8, 80, 256), BF),
        v((8, 64, 256), BF),
        v((512, 1024), BF),
        v((512, 1024), BF),
        v((512, 1024), BF),
        v((64, 2048), BF),
        v((8, 64, 2048), BF),
        v((8, 64, 256), BF),
        v((512, 2048), BF),
        dma((10,)),
        dma((2, 18)), dma((2, 18)), dma((18,)), dma((18,)), dma((2, 18)), dma((2, 18)), dma((14,)), dma((14,)),
        dma((3,)), dma((3,)),
        dma((8, 8)), dma((8, 8)), dma((8, 8)), dma((8, 8)),
        dma((2, 8)), dma((2, 8)), dma((2, 8)), dma((2, 8)),
        dma((6, 8)), dma((6, 8)),
        dma((1,)), dma((8,)), dma((8,)), dma((1,)),
    ]
    return pl.pallas_call(
        kernel,
        out_shape=jax.ShapeDtypeStruct((512, 512), BF),
        in_specs=[any_, vmem, any_, smem, smem, any_, any_, any_, any_, any_, any_],
        out_specs=vmem,
        scratch_shapes=scratch,
        compiler_params=pltpu.CompilerParams(
            collective_id=0, has_side_effects=True, vmem_limit_bytes=58 << 20
        ),
        cost_estimate=pl.CostEstimate(flops=11_000_000_000, bytes_accessed=14_000_000, transcendentals=1_000_000),
    )(
        hidden, gain, trace.reshape(8, 64, 128), counts, offsets.T,
        w_skv, w_eq, w_eo, w_cq, w_ckv, w_co,
    )


def solution(mesh):
    place = ("seq", "section")
    in_specs = (
        P(place, "tp"), P(), P(place, "tp"), P(place), P(place, None), P(None, "tp"),
        P("section", None), P("section", None), P(None, "tp"), P(None, "tp"), P("tp", None),
    )
    return jax.shard_map(body, mesh=mesh, in_specs=in_specs, out_specs=P(place, "tp"), check_vma=False)
```

```python
import functools
import math

import jax
import jax.numpy as jnp
from jax import lax
from jax.experimental import pallas as pl
from jax.experimental.pallas import tpu as pltpu
from jax.sharding import PartitionSpec as P

MESH = pl.DeviceIdType.MESH
BF = jnp.bfloat16
F32 = jnp.float32
EPS = 1e-05
NEG = -1e30
FACTOR = 1.0 / math.sqrt(128)
TP = 8
PLACES = 32


def remote(src, dst, send, recv, to):
    return pltpu.make_async_remote_copy(
        src_ref=src, dst_ref=dst, send_sem=send, recv_sem=recv, device_id=to, device_id_type=MESH
    )


def dot(a, b):
    return jnp.dot(a, b, preferred_element_type=F32)


def dot_t(a, b):
    return lax.dot_general(a, b, (((1,), (1,)), ((), ())), preferred_element_type=F32)


class Here:
    def __init__(self):
        self.c = lax.axis_index("seq")
        self.t = lax.axis_index("tp")
        self.s = lax.axis_index("section")
        self.y, self.xl = self.t // 2, self.t % 2
        self.z, self.xh = self.s // 2, self.s % 2
        self.p = self.c * 16 + self.s
        c, t, s = self.c, self.t, self.s
        self.yp = (c, self.slot(1, 0), s)
        self.ym = (c, self.slot(3, 0), s)
        self.xp = (c, self.slot(0, 1), s)
        self.zp = (c, t, ((self.z + 1) % 8) * 2 + self.xh)
        self.zm = (c, t, ((self.z + 7) % 8) * 2 + self.xh)
        self.x2 = (c, t, self.z * 2 + 1 - self.xh)
        self.xo = (c, self.slot(0, 1), self.z * 2 + 1 - self.xh)
        self.core = (1 - c, t, s)
        before, after = (self.p + PLACES - 1) % PLACES, (self.p + 1) % PLACES
        self.before = (before // 16, before % 16)
        self.after = (after // 16, after % 16)

    def slot(self, dy, other):
        xl = 1 - self.xl if other else self.xl
        return ((self.y + dy) % 4) * 2 + xl

    def tp_peer(self, i):
        return (self.t + i) % TP

    def any_copy(self, dy, other):
        return (self.c, self.slot(dy, other), self.z * 2 + (1 - self.xh if other else self.xh))

    def at_tp(self, t):
        return (self.c, t, self.s)

    def last_before(self):
        return (self.before[0], TP - 1, self.before[1])

    def at_after(self, t):
        return (self.after[0], t, self.after[1])


class Gather:
    def __init__(self, here, region, own, send, recv, arrived, xp):
        self.here, self.region, self.own, self.xp = here, region, own, xp
        self.send_sem, self.recv_sem, self.arrived = send, recv, arrived
        self.sent = []

    def send(self, m, to, slot, part, half=None, own=False):
        src = self.own(part) if own else self.region(slot, part, half)
        copy = remote(src, self.region(slot, part, half), self.send_sem.at[m], self.recv_sem.at[m], to)
        copy.start()
        self.sent.append(copy)

    def wait(self, m, slot, part, half=None):
        ref = self.region(slot, part, half)
        remote(ref, ref, self.send_sem.at[m], self.recv_sem.at[m], self.xp).wait_recv()

    def begin(self, part):
        if part == 0:
            self.begin_x(0)
            self.begin_y(0)
        else:
            self.begin_y(1)
            self.begin_x(1)

    def begin_x(self, part):
        self.send(3 * part, self.xp, self.here.t, part, own=True)

    def begin_y(self, part):
        h = self.here
        self.send(3 * part + 1, h.yp, h.t, part, own=True)
        self.send(3 * part + 2, h.ym, h.t, part, own=True)

    def steps(self):
        h = self.here
        slot = h.slot
        self.wait(0, slot(0, 1), 0)
        self.send(6, h.yp, slot(0, 1), 0)
        self.send(7, h.ym, slot(0, 1), 0)
        self.arrived(slot(0, 1), 0, 0)
        yield
        self.wait(4, slot(3, 0), 1)
        self.send(12, self.xp, slot(3, 0), 1)
        self.send(14, h.yp, slot(3, 0), 1, 0)
        self.arrived(slot(3, 0), 1, 1)
        yield
        self.wait(5, slot(1, 0), 1)
        self.send(13, self.xp, slot(1, 0), 1)
        self.send(15, h.ym, slot(1, 0), 1, 1)
        self.arrived(slot(1, 0), 1, 2)
        yield
        self.wait(1, slot(3, 0), 0)
        self.send(8, h.yp, slot(3, 0), 0, 0)
        self.arrived(slot(3, 0), 0, 3)
        yield
        self.wait(2, slot(1, 0), 0)
        self.send(9, h.ym, slot(1, 0), 0, 1)
        self.arrived(slot(1, 0), 0, 4)
        yield
        self.wait(3, slot(0, 1), 1)
        self.arrived(slot(0, 1), 1, 5)
        yield
        self.wait(14, slot(2, 0), 1, 0)
        self.send(16, self.xp, slot(2, 0), 1, 0)
        self.wait(15, slot(2, 0), 1, 1)
        self.send(17, self.xp, slot(2, 0), 1, 1)
        self.arrived(slot(2, 0), 1, 6)
        yield
        self.wait(6, slot(3, 1), 0)
        self.send(10, h.yp, slot(3, 1), 0, 0)
        self.arrived(slot(3, 1), 0, 7)
        yield
        self.wait(7, slot(1, 1), 0)
        self.send(11, h.ym, slot(1, 1), 0, 1)
        self.arrived(slot(1, 1), 0, 8)
        yield
        self.wait(8, slot(2, 0), 0, 0)
        self.wait(9, slot(2, 0), 0, 1)
        self.arrived(slot(2, 0), 0, 9)
        yield
        self.wait(12, slot(3, 1), 1)
        self.arrived(slot(3, 1), 1, 10)
        yield
        self.wait(13, slot(1, 1), 1)
        self.arrived(slot(1, 1), 1, 11)
        yield
        self.wait(10, slot(2, 1), 0, 0)
        self.wait(11, slot(2, 1), 0, 1)
        self.arrived(slot(2, 1), 0, 12)
        yield
        self.wait(16, slot(2, 1), 1, 0)
        self.wait(17, slot(2, 1), 1, 1)
        self.arrived(slot(2, 1), 1, 13)

    def order(self):
        s = self.here.slot
        return [
            (s(0, 1), 0), (s(3, 0), 1), (s(1, 0), 1), (s(3, 0), 0), (s(1, 0), 0), (s(0, 1), 1), (s(2, 0), 1),
            (s(3, 1), 0), (s(1, 1), 0), (s(2, 0), 0), (s(3, 1), 1), (s(1, 1), 1), (s(2, 1), 0), (s(2, 1), 1),
        ]

    def finish(self):
        for copy in self.sent:
            copy.wait_send()


class Ring:
    OFFSET = [0, 7, 1, 6, 2, 5, 3, 4]

    def __init__(self, here, region, sems, flip, cross=None):
        self.here, self.region, self.flip, self.cross = here, region, flip, cross
        self.send_sem, self.recv_sem, self.core_send, self.core_recv = sems
        self.sent = []

    def push(self, way, r):
        h = self.here
        z = (h.z + (8 - r if way == 0 else r)) % 8
        ref = self.region(z, h.c)
        m = way * 4 + r
        copy = remote(ref, ref, self.send_sem.at[m], self.recv_sem.at[m], h.zp if way == 0 else h.zm)
        copy.start()
        self.sent.append(copy)

    def share(self, k):
        h = self.here
        ref = self.region((h.z + self.dz(k)) % 8, h.c)
        copy = remote(ref, ref, self.core_send.at[k], self.core_recv.at[k], h.core)
        copy.start()
        self.sent.append(copy)
        if self.cross:
            copy = remote(ref, ref, self.cross[0].at[k], self.cross[1].at[k], h.xo)
            copy.start()
            self.sent.append(copy)

    def swap(self):
        h = self.here
        for k in range(8):
            ref = self.region((h.z + self.dz(k)) % 8, h.c, 1 - h.xh)
            remote(ref, ref, self.cross[0].at[k], self.cross[1].at[k], h.xo).wait_recv()
            copy = remote(ref, ref, self.cross[2].at[k], self.cross[3].at[k], h.core)
            copy.start()
            self.sent.append(copy)
            yield

    def dz(self, k):
        return self.OFFSET[k] if not self.flip else (8 - self.OFFSET[k]) % 8

    def wait(self, way, r, k):
        h = self.here
        ref = self.region((h.z + self.dz(k)) % 8, h.c)
        m = way * 4 + r
        remote(ref, ref, self.send_sem.at[m], self.recv_sem.at[m], h.zp).wait_recv()

    def steps(self):
        first, second = (1, 0) if self.flip else (0, 1)
        self.push(first, 0)
        self.push(second, 0)
        self.share(0)
        yield
        for r in range(3):
            self.wait(first, r, 1 + 2 * r)
            self.push(first, r + 1)
            self.share(1 + 2 * r)
            self.wait(second, r, 2 + 2 * r)
            if r < 2:
                self.push(second, r + 1)
            self.share(2 + 2 * r)
            yield
        self.wait(first, 3, 7)
        self.share(7)
        yield

    def collect(self):
        h = self.here
        for k in range(8):
            ref = self.region((h.z + self.dz(k)) % 8, 1 - h.c)
            remote(ref, ref, self.core_send.at[k], self.core_recv.at[k], h.core).wait_recv()
            if self.cross:
                ref = self.region((h.z + self.dz(k)) % 8, 1 - h.c, 1 - h.xh)
                remote(ref, ref, self.cross[2].at[k], self.cross[3].at[k], h.core).wait_recv()

    def finish(self):
        for copy in self.sent:
            copy.wait_send()


def advance(steps, n=1):
    for _ in range(n):
        next(steps, None)


def kernel(
    hidden, gain_in, trace, counts, offsets, w_skv, w_eq, w_eo, w_cq, w_ckv, w_co, out,
    gain, hid, wproj, acc, ssq, kv_s, q_s, tr, picked, rows, enc_w, wck, woc, kvx, qx, qh, eq, ea, enc,
    att_own, attg, tail, attb,
    local, h_send, h_recv, k_send, k_recv, a_send, a_recv, kc_send, kc_recv,
    x_send, x_recv, r_ss, r_rs, r_cs, r_cr, s_xs, s_xr, s_cs, s_cr,
    p_send, p_recv, halo_send, halo_recv, tail_send, tail_recv,
):
    h = Here()
    c, t, s, z, xh, p = h.c, h.t, h.s, h.z, h.xh, h.p
    is_last = t == TP - 1

    barrier = pltpu.get_barrier_semaphore()
    greet = [h.at_tp(h.tp_peer(i)) for i in range(1, TP)]
    greet += [h.any_copy(dy, 1) for dy in range(4)]
    greet += [h.zp, h.zm, h.x2, h.core, h.last_before()]
    for device in greet:
        pl.semaphore_signal(barrier, inc=1, device_id=device, device_id_type=MESH)

    @pl.when(is_last)
    def _():
        for other in range(TP):
            pl.semaphore_signal(barrier, inc=1, device_id=h.at_after(other), device_id_type=MESH)

    pl.semaphore_wait(barrier, len(greet) + TP * (t // (TP - 1)))

    pushes = []

    def push(src, dst, send, recv, to):
        copy = remote(src, dst, send, recv, to)
        copy.start()
        pushes.append(copy)

    def came(ref, recv):
        remote(ref, ref, p_send.at[0, 0], recv, h.core).wait_recv()

    def bring(src, dst, i):
        copy = pltpu.make_async_copy(src, dst, local.at[i])
        copy.start()
        return copy

    def project(slot, part, index):
        here = pl.ds(part * 256, 256)
        wide = hid[slot, here, :].astype(F32)
        squares = jnp.sum(wide * wide, axis=-1, keepdims=True)
        scaled = (wide * gain[slot]).astype(BF)
        w = wproj[pl.ds(pl.multiple_of(slot * 512, 512), 512), :]
        product = dot(scaled, w)
        if index is None:
            ssq[here, :] = squares
            acc[here, :] = product
        else:
            ssq[here, :] += squares
            acc[here, :] += product

    def hid_gather(i):
        def region(slot, part, half):
            base = part * 256 + i * 128
            if half is None:
                return hid.at[slot, pl.ds(base, 128)]
            return hid.at[slot, pl.ds(base + half * 64, 64)]

        def own(part):
            return hidden.at[pl.ds(part * 256 + i * 128, 128)]

        def arrived(slot, part, index):
            if i == 1:
                project(slot, part, index)

        return Gather(h, region, own, h_send.at[i], h_recv.at[i], arrived, h.xp)

    gather_h = [hid_gather(0), hid_gather(1)]
    for g in gather_h:
        g.begin(0)
        g.begin(1)
    steps_h = [g.steps() for g in gather_h]

    mine = pl.ds(p * 8, 8)
    halves = pl.ds(c * 32, 32)
    push(trace, tr.at[mine], x_send.at[0], x_recv.at[0], h.x2)
    own_trace = bring(trace, tr.at[mine], 0)
    own_hid = bring(hidden, hid.at[t], 1)
    own_skv = bring(w_skv, wproj.at[:, pl.ds(0, 256)], 2)
    own_cq = bring(w_cq, wproj.at[:, pl.ds(256, 256)], 3)
    own_eq = bring(w_eq.at[halves], enc_w.at[0, s, c], 4)
    own_eo = bring(w_eo.at[halves], enc_w.at[1, s, c], 5)
    own_ckv = [bring(w_ckv.at[pl.ds(512 * i, 256)], wck.at[t, pl.ds(512 * i, 256)], 6 + i) for i in range(2)]
    ck_rows = pl.ds(c * 512 + 256 + z * 32, 32)
    own_ckv.append(bring(w_ckv.at[ck_rows], wck.at[t, ck_rows], 8))
    co_rows = pl.ds(z * 32 + c * 16, 16)
    own_co = bring(w_co.at[co_rows, pl.ds(pl.multiple_of(t * 512, 512), 512)], woc.at[t, z * 2 + c], 9)

    def ring(i, region, flip):
        return Ring(h, region, (r_ss.at[i], r_rs.at[i], r_cs.at[i], r_cr.at[i]), flip)

    def trace_ring(i, sel):
        return ring(i, lambda zz, cc: tr.at[pl.ds((cc * 16 + zz * 2 + sel) * 8, 8)], bool(i % 2))

    def enc_ring(i):
        w = i % 2
        return Ring(
            h, lambda zz, cc, sel=xh: enc_w.at[w, zz * 2 + sel, cc],
            (r_ss.at[i], r_rs.at[i], r_cs.at[i], r_cr.at[i]), bool(w),
            (s_xs.at[w], s_xr.at[w], s_cs.at[w], s_cr.at[w]),
        )

    def ckv_ring(i):
        return ring(
            i, lambda zz, cc: wck.at[pl.ds(4 * (i % 2), 4), pl.ds(cc * 512 + 256 + zz * 32, 32)], bool(i % 2)
        )

    def co_ring(i):
        return ring(i, lambda zz, cc: woc.at[pl.ds(4 * (i % 2), 4), zz * 2 + cc], bool(i % 2))

    rings_t = [trace_ring(0, xh), trace_ring(1, 1 - xh)]
    rings_e = [enc_ring(2), enc_ring(3)]
    rings_k = [ckv_ring(4), ckv_ring(5)]
    rings_o = [co_ring(6), co_ring(7)]
    rings = rings_t + rings_e + rings_k + rings_o
    steps_t, steps_e, steps_k2, steps_o = (
        [r.steps() for r in group] for group in (rings_t, rings_e, rings_k, rings_o)
    )

    own_trace.wait()
    advance(steps_t[0])
    came(tr.at[pl.ds((p + 1 - 2 * xh) * 8, 8)], x_recv.at[0])
    advance(steps_t[1])

    def wck_region(slot, part, half):
        base = c * 512 + part * 128
        if half is None:
            return wck.at[slot, pl.ds(base, 128)]
        return wck.at[slot, pl.ds(base + half * 64, 64)]

    def share(slot, part, index):
        ref = wck_region(slot, part, None)
        push(ref, ref, kc_send.at[index], kc_recv.at[index], h.core)

    gather_k = Gather(
        h, wck_region, lambda part: w_ckv.at[pl.ds(c * 512 + part * 128, 128)], k_send, k_recv, share, h.xo
    )
    gather_k.begin_x(0)
    gather_k.begin_x(1)
    steps_k = gather_k.steps()

    others = [(0, 1), (1, 0), (3, 0), (1, 1), (3, 1), (2, 0), (2, 1)]
    for i, (dy, other) in enumerate(others):
        push(w_ckv.at[ck_rows], wck.at[t, ck_rows], p_send.at[0, i], p_recv.at[0, i], h.any_copy(dy, other))
    for i, (dy, other) in enumerate(others):
        cols = pl.ds(pl.multiple_of(h.slot(dy, other) * 512, 512), 512)
        push(
            w_co.at[co_rows, cols], woc.at[t, z * 2 + c], p_send.at[1, i], p_recv.at[1, i],
            h.any_copy(dy, other),
        )

    for i in range(TP):
        gain[i] = gain_in[512 * i : 512 * (i + 1)].astype(F32).reshape(1, 512)
    own_hid.wait()
    own_skv.wait()
    own_cq.wait()
    project(t, 0, None)
    project(t, 1, None)

    def both(steps, n=1):
        for _ in range(n):
            for one in steps:
                advance(one)

    both(steps_h, 2)
    both(steps_t)
    both(steps_h, 3)
    both(steps_t)
    own_eq.wait()
    own_eo.wait()
    both(steps_e)
    both(steps_h, 3)
    both(steps_t)
    both(steps_e)
    both(steps_h, 2)
    both(steps_t)

    for r in rings_t:
        r.collect()

    def pick(owner):
        for k in range(4):
            at = p * 8 + owner - offsets[k, owner]
            at = jnp.minimum(jnp.maximum(at, 0), 254)
            picked[owner, 128 * k : 128 * k + 64, :] = tr[at]
            picked[owner, 128 * k + 64 : 128 * k + 128, :] = tr[at + 1]

    columns = pl.ds(pl.multiple_of(t * 128, 128), 128)
    for i in range(1, TP):
        to = h.tp_peer(i)
        pick(to)
        push(picked.at[to], rows.at[:, columns], p_send.at[3, i], p_recv.at[3, i], h.at_tp(to))
    pick(t)
    rows[:, columns] = picked[t]

    both(steps_h, 2)
    both(steps_e)
    for copy in own_ckv:
        copy.wait()
    for i, (dy, other) in enumerate(others):
        came(wck.at[h.slot(4 - dy, other), ck_rows], p_recv.at[0, i])
    both(steps_k2)
    both(steps_h, 2)

    inverse = lax.rsqrt(ssq[...] * (1.0 / 4096) + EPS)
    projected = (acc[...] * inverse).astype(BF)
    kv_s[...] = projected[:, :256]
    q_s[0:512, :] = projected[:, 256:]
    q_s[512:576, :] = jnp.zeros((64, 256), BF)
    for i in range(1, TP):
        to = h.tp_peer(i)
        mine_there = pl.ds(pl.multiple_of(to * 64, 64), 64)
        push(kv_s.at[mine_there], kvx.at[t], p_send.at[2, i], p_recv.at[2, i], h.at_tp(to))
    kvx[t] = kv_s[pl.ds(pl.multiple_of(t * 64, 64), 64), :]

    for i in range(1, TP):
        to = h.tp_peer(i)
        mine_there = pl.ds(pl.multiple_of(to * 64 + 48, 16), 80)
        push(q_s.at[mine_there], qx.at[t], p_send.at[4, i], p_recv.at[4, i], h.at_tp(to))
    qx[t] = q_s[pl.ds(pl.multiple_of(t * 64 + 48, 16), 80), :]
    push(q_s.at[pl.ds(0, 64)], qh.at[t], halo_send.at[0], halo_recv.at[t], h.last_before())

    gather_k.begin_y(1)
    gather_k.begin_y(0)
    both(steps_e)
    swaps = [r.swap() for r in rings_e]
    both(swaps, 3)
    both(steps_e)
    both(swaps, 2)
    both(steps_k2)
    own_co.wait()
    for i, (dy, other) in enumerate(others):
        came(woc.at[h.slot(4 - dy, other), z * 2 + c], p_recv.at[1, i])

    def from_peer(i):
        return h.tp_peer(TP - i)

    for i in range(1, TP):
        cols = pl.ds(pl.multiple_of(from_peer(i) * 128, 128), 128)
        came(rows.at[:, cols], p_recv.at[3, i])
    advance(steps_k, 1)
    both(swaps, 3)
    both(steps_k2)
    for r in rings_e:
        r.collect()
    for n in range(4):
        cols = slice(256 * n, 256 * (n + 1))
        eq[:, cols] = dot(rows[...], enc_w[0, :, :, :, cols].reshape(1024, 256)).astype(BF)
    advance(steps_k, 2)
    both(steps_k2)
    for i in range(1, TP):
        came(kvx.at[from_peer(i)], p_recv.at[2, i])
    advance(steps_k, 2)
    for e in range(8):
        cols = slice(128 * e, 128 * (e + 1))
        scores = dot_t(eq[:, cols], kvx[e, :, :128]) * FACTOR
        top = jnp.max(scores, axis=-1, keepdims=True)
        weights = jnp.exp(scores - top)
        probs = (weights * (1.0 / jnp.sum(weights, axis=-1, keepdims=True))).astype(BF)
        ea[:, cols] = dot(probs, kvx[e, :, 128:]).astype(BF)
        advance(steps_k, 1)
        if e == 3:
            both(steps_k2)
            both(steps_o)
    for n in range(4):
        cols = slice(256 * n, 256 * (n + 1))
        update = dot(ea[...], enc_w[1, :, :, :, cols].reshape(1024, 256))
        enc[:, cols] = (rows[:, cols].astype(F32) + update).astype(BF)
        advance(steps_k, 1)
    both(steps_k2)
    both(steps_o)

    for i in range(1, TP):
        came(qx.at[from_peer(i)], p_recv.at[4, i])

    @pl.when(is_last)
    def _():
        for j in range(TP):
            came(qh.at[j], halo_recv.at[j])
            qx[j, 16:80, :] = qh[j]

    for index, (slot, part) in enumerate(gather_k.order()):
        came(wck.at[slot, pl.ds((1 - c) * 512 + part * 128, 128)], kc_recv.at[index])
    for r in rings_k:
        r.collect()

    live_keys = counts[t] * 128
    mask = lax.broadcasted_iota(jnp.int32, (160, 512), 1) < live_keys
    any_live = jnp.zeros((64, 128), jnp.int32) + live_keys > 0
    last_row = lax.broadcasted_iota(jnp.int32, (64, 128), 0) == 63

    def att_gather(i):
        def region(slot, part, half):
            base = i * 1024 + part * 512
            if half is None:
                return attg.at[slot, :, pl.ds(base, 512)]
            return attg.at[slot, :, pl.ds(base + half * 256, 256)]

        def own(part):
            return att_own.at[:, pl.ds(i * 1024 + part * 512, 512)]

        return Gather(h, region, own, a_send.at[i], a_recv.at[i], lambda *_: None, h.xp)

    gather_a = [att_gather(0), att_gather(1)]
    steps_a = [g.steps() for g in gather_a]

    def tail_copy(j):
        return remote(
            att_own.at[:, pl.ds(256 * j, 256)], tail.at[j],
            tail_send.at[j], tail_recv.at[0], h.at_after(j),
        )

    for j in range(TP):
        pair = dot(enc[...], wck[j]).astype(BF)
        scores = jnp.concatenate(
            [dot_t(qx[j, :, 128 * i : 128 * i + 128], pair[:, 256 * i : 256 * i + 128]) for i in range(2)], axis=0
        )
        scores = jnp.where(mask, scores * FACTOR, NEG)
        weights = jnp.exp(scores - jnp.max(scores, axis=-1, keepdims=True))
        probs = (weights * (1.0 / jnp.sum(weights, axis=-1, keepdims=True))).astype(BF)
        for i in range(2):
            mixed = dot(probs[80 * i : 80 * i + 80], pair[:, 256 * i + 128 : 256 * i + 256])
            mixed = jnp.where(last_row, mixed[15:16], mixed[16:80])
            at = 256 * j + 128 * i
            att_own[:, at : at + 128] = jnp.where(any_live, mixed, 0.0).astype(BF)

        @pl.when(is_last)
        def _():
            tail_copy(j).start()

        if j == 1:
            gather_a[0].begin(0)
        if j == 3:
            gather_a[0].begin(1)
            both(steps_o)
        if j == 3:
            advance(steps_a[0], 1)
        if j == 5:
            advance(steps_a[0], 2)
        if j == 5:
            gather_a[1].begin(0)
            both(steps_o)
        if j == 6:
            advance(steps_a[0], 2)
        if j == 7:
            advance(steps_a[0], 1)
    gather_a[1].begin(1)
    advance(steps_a[1], 1)
    advance(steps_a[0], 1)
    both(steps_o)
    came(tail.at[t], tail_recv.at[0])
    for i in range(1, TP):
        push(tail.at[t], tail.at[t], p_send.at[5, i], p_recv.at[5, i], h.at_tp(h.tp_peer(i)))
    advance(steps_a[0], 1)
    advance(steps_a[1], 2)
    advance(steps_a[0], 2)
    advance(steps_a[1], 2)
    advance(steps_a[0], 3)
    advance(steps_a[1], 3)
    advance(steps_a[0], 2)
    attg[t] = att_own[...]
    for i in range(1, TP):
        came(tail.at[from_peer(i)], p_recv.at[5, i])
    for r in rings_o:
        r.collect()

    own_row = lax.broadcasted_iota(jnp.int32, (16, 1024), 0) == 15

    def attended(i):
        cols = slice(1024 * i, 1024 * (i + 1))
        for j in range(4 * i, 4 * i + 4):
            attb[0:64, 256 * j : 256 * (j + 1)] = jnp.where(p > 0, tail[j].astype(F32), 0.0).astype(BF)
        for v in range(TP):
            if v:
                attb[64 * v : 64 * v + 64, cols] = attg[v - 1, :, cols]
            attb[64 * v + 48 : 64 * v + 64, cols] = jnp.where(
                own_row, attg[v, 48:64, cols], attb[64 * v + 48 : 64 * v + 64, cols]
            )
        return dot(attb[:, cols], woc[4 * i : 4 * i + 4].reshape(1024, 512))

    acc[...] = hid[t].astype(F32) + attended(0)
    advance(steps_a[1], 7)
    out[...] = (acc[...] + attended(1)).astype(BF)

    for group in gather_h + [gather_k] + gather_a + rings:
        group.finish()
    for copy in pushes:
        copy.wait_send()

    @pl.when(is_last)
    def _():
        for j in range(TP):
            tail_copy(j).wait_send()


def body(hidden, gain, trace, counts, offsets, w_skv, w_eq, w_eo, w_cq, w_ckv, w_co):
    any_ = pl.BlockSpec(memory_space=pl.ANY)
    vmem = pl.BlockSpec(memory_space=pltpu.VMEM)
    smem = pl.BlockSpec(memory_space=pltpu.SMEM)
    dma = pltpu.SemaphoreType.DMA
    v = pltpu.VMEM
    scratch = [
        v((8, 1, 512), F32),
        v((8, 512, 512), BF),
        v((4096, 512), BF),
        v((512, 512), F32),
        v((512, 1), F32),
        v((512, 256), BF),
        v((576, 256), BF),
        v((256, 64, 128), BF),
        v((8, 512, 128), BF),
        v((512, 1024), BF),
        v((2, 16, 2, 32, 1024), BF),
        v((8, 1024, 512), BF),
        v((8, 16, 16, 512), BF),
        v((8, 64, 256), BF),
        v((8, 80, 256), BF),
        v((8, 64, 256), BF),
        v((512, 1024), BF),
        v((512, 1024), BF),
        v((512, 1024), BF),
        v((64, 2048), BF),
        v((8, 64, 2048), BF),
        v((8, 64, 256), BF),
        v((512, 2048), BF),
        dma((10,)),
        dma((2, 18)), dma((2, 18)), dma((18,)), dma((18,)), dma((2, 18)), dma((2, 18)), dma((14,)), dma((14,)),
        dma((3,)), dma((3,)),
        dma((8, 8)), dma((8, 8)), dma((8, 8)), dma((8, 8)),
        dma((2, 8)), dma((2, 8)), dma((2, 8)), dma((2, 8)),
        dma((6, 8)), dma((6, 8)),
        dma((1,)), dma((8,)), dma((8,)), dma((1,)),
    ]
    return pl.pallas_call(
        kernel,
        out_shape=jax.ShapeDtypeStruct((512, 512), BF),
        in_specs=[any_, vmem, any_, smem, smem, any_, any_, any_, any_, any_, any_],
        out_specs=vmem,
        scratch_shapes=scratch,
        compiler_params=pltpu.CompilerParams(
            collective_id=0, has_side_effects=True, vmem_limit_bytes=58 << 20
        ),
        cost_estimate=pl.CostEstimate(flops=11_000_000_000, bytes_accessed=14_000_000, transcendentals=1_000_000),
    )(
        hidden, gain, trace.reshape(8, 64, 128), counts, offsets.T,
        w_skv, w_eq, w_eo, w_cq, w_ckv, w_co,
    )


def solution(mesh):
    place = ("seq", "section")
    in_specs = (
        P(place, "tp"), P(), P(place, "tp"), P(place), P(place, None), P(None, "tp"),
        P("section", None), P("section", None), P(None, "tp"), P(None, "tp"), P("tp", None),
    )
    return jax.shard_map(body, mesh=mesh, in_specs=in_specs, out_specs=P(place, "tp"), check_vma=False)
```

```python
import functools
import math

import jax
import jax.numpy as jnp
from jax import lax
from jax.experimental import pallas as pl
from jax.experimental.pallas import tpu as pltpu
from jax.sharding import PartitionSpec as P

MESH = pl.DeviceIdType.MESH
BF = jnp.bfloat16
F32 = jnp.float32
EPS = 1e-05
NEG = -1e30
FACTOR = 1.0 / math.sqrt(128)
TP = 8
PLACES = 32


def remote(src, dst, send, recv, to):
    return pltpu.make_async_remote_copy(
        src_ref=src, dst_ref=dst, send_sem=send, recv_sem=recv, device_id=to, device_id_type=MESH
    )


def dot(a, b):
    return jnp.dot(a, b, preferred_element_type=F32)


def dot_t(a, b):
    return lax.dot_general(a, b, (((1,), (1,)), ((), ())), preferred_element_type=F32)


class Here:
    def __init__(self):
        self.c = lax.axis_index("seq")
        self.t = lax.axis_index("tp")
        self.s = lax.axis_index("section")
        self.y, self.xl = self.t // 2, self.t % 2
        self.z, self.xh = self.s // 2, self.s % 2
        self.p = self.c * 16 + self.s
        c, t, s = self.c, self.t, self.s
        self.yp = (c, self.slot(1, 0), s)
        self.ym = (c, self.slot(3, 0), s)
        self.xp = (c, self.slot(0, 1), s)
        self.zp = (c, t, ((self.z + 1) % 8) * 2 + self.xh)
        self.zm = (c, t, ((self.z + 7) % 8) * 2 + self.xh)
        self.x2 = (c, t, self.z * 2 + 1 - self.xh)
        self.xo = (c, self.slot(0, 1), self.z * 2 + 1 - self.xh)
        self.core = (1 - c, t, s)
        before, after = (self.p + PLACES - 1) % PLACES, (self.p + 1) % PLACES
        self.before = (before // 16, before % 16)
        self.after = (after // 16, after % 16)

    def slot(self, dy, other):
        xl = 1 - self.xl if other else self.xl
        return ((self.y + dy) % 4) * 2 + xl

    def tp_peer(self, i):
        return (self.t + i) % TP

    def any_copy(self, dy, other):
        return (self.c, self.slot(dy, other), self.z * 2 + (1 - self.xh if other else self.xh))

    def at_tp(self, t):
        return (self.c, t, self.s)

    def last_before(self):
        return (self.before[0], TP - 1, self.before[1])

    def at_after(self, t):
        return (self.after[0], t, self.after[1])


class Gather:
    def __init__(self, here, region, own, send, recv, arrived, xp):
        self.here, self.region, self.own, self.xp = here, region, own, xp
        self.send_sem, self.recv_sem, self.arrived = send, recv, arrived
        self.sent = []

    def send(self, m, to, slot, part, half=None, own=False):
        src = self.own(part) if own else self.region(slot, part, half)
        copy = remote(src, self.region(slot, part, half), self.send_sem.at[m], self.recv_sem.at[m], to)
        copy.start()
        self.sent.append(copy)

    def wait(self, m, slot, part, half=None):
        ref = self.region(slot, part, half)
        remote(ref, ref, self.send_sem.at[m], self.recv_sem.at[m], self.xp).wait_recv()

    def begin(self, part):
        if part == 0:
            self.begin_x(0)
            self.begin_y(0)
        else:
            self.begin_y(1)
            self.begin_x(1)

    def begin_x(self, part):
        self.send(3 * part, self.xp, self.here.t, part, own=True)

    def begin_y(self, part):
        h = self.here
        self.send(3 * part + 1, h.yp, h.t, part, own=True)
        self.send(3 * part + 2, h.ym, h.t, part, own=True)

    def steps(self):
        h = self.here
        slot = h.slot
        self.wait(0, slot(0, 1), 0)
        self.send(6, h.yp, slot(0, 1), 0)
        self.send(7, h.ym, slot(0, 1), 0)
        self.arrived(slot(0, 1), 0, 0)
        yield
        self.wait(4, slot(3, 0), 1)
        self.send(12, self.xp, slot(3, 0), 1)
        self.send(14, h.yp, slot(3, 0), 1, 0)
        self.arrived(slot(3, 0), 1, 1)
        yield
        self.wait(5, slot(1, 0), 1)
        self.send(13, self.xp, slot(1, 0), 1)
        self.send(15, h.ym, slot(1, 0), 1, 1)
        self.arrived(slot(1, 0), 1, 2)
        yield
        self.wait(1, slot(3, 0), 0)
        self.send(8, h.yp, slot(3, 0), 0, 0)
        self.arrived(slot(3, 0), 0, 3)
        yield
        self.wait(2, slot(1, 0), 0)
        self.send(9, h.ym, slot(1, 0), 0, 1)
        self.arrived(slot(1, 0), 0, 4)
        yield
        self.wait(3, slot(0, 1), 1)
        self.arrived(slot(0, 1), 1, 5)
        yield
        self.wait(14, slot(2, 0), 1, 0)
        self.send(16, self.xp, slot(2, 0), 1, 0)
        self.wait(15, slot(2, 0), 1, 1)
        self.send(17, self.xp, slot(2, 0), 1, 1)
        self.arrived(slot(2, 0), 1, 6)
        yield
        self.wait(6, slot(3, 1), 0)
        self.send(10, h.yp, slot(3, 1), 0, 0)
        self.arrived(slot(3, 1), 0, 7)
        yield
        self.wait(7, slot(1, 1), 0)
        self.send(11, h.ym, slot(1, 1), 0, 1)
        self.arrived(slot(1, 1), 0, 8)
        yield
        self.wait(8, slot(2, 0), 0, 0)
        self.wait(9, slot(2, 0), 0, 1)
        self.arrived(slot(2, 0), 0, 9)
        yield
        self.wait(12, slot(3, 1), 1)
        self.arrived(slot(3, 1), 1, 10)
        yield
        self.wait(13, slot(1, 1), 1)
        self.arrived(slot(1, 1), 1, 11)
        yield
        self.wait(10, slot(2, 1), 0, 0)
        self.wait(11, slot(2, 1), 0, 1)
        self.arrived(slot(2, 1), 0, 12)
        yield
        self.wait(16, slot(2, 1), 1, 0)
        self.wait(17, slot(2, 1), 1, 1)
        self.arrived(slot(2, 1), 1, 13)

    def order(self):
        s = self.here.slot
        return [
            (s(0, 1), 0), (s(3, 0), 1), (s(1, 0), 1), (s(3, 0), 0), (s(1, 0), 0), (s(0, 1), 1), (s(2, 0), 1),
            (s(3, 1), 0), (s(1, 1), 0), (s(2, 0), 0), (s(3, 1), 1), (s(1, 1), 1), (s(2, 1), 0), (s(2, 1), 1),
        ]

    def finish(self):
        for copy in self.sent:
            copy.wait_send()


class Ring:
    OFFSET = [0, 7, 1, 6, 2, 5, 3, 4]

    def __init__(self, here, region, sems, flip, cross=None):
        self.here, self.region, self.flip, self.cross = here, region, flip, cross
        self.send_sem, self.recv_sem, self.core_send, self.core_recv = sems
        self.sent = []

    def push(self, way, r):
        h = self.here
        z = (h.z + (8 - r if way == 0 else r)) % 8
        ref = self.region(z, h.c)
        m = way * 4 + r
        copy = remote(ref, ref, self.send_sem.at[m], self.recv_sem.at[m], h.zp if way == 0 else h.zm)
        copy.start()
        self.sent.append(copy)

    def share(self, k):
        h = self.here
        ref = self.region((h.z + self.dz(k)) % 8, h.c)
        copy = remote(ref, ref, self.core_send.at[k], self.core_recv.at[k], h.core)
        copy.start()
        self.sent.append(copy)
        if self.cross:
            copy = remote(ref, ref, self.cross[0].at[k], self.cross[1].at[k], h.xo)
            copy.start()
            self.sent.append(copy)

    def swap(self):
        h = self.here
        for k in range(8):
            ref = self.region((h.z + self.dz(k)) % 8, h.c, 1 - h.xh)
            remote(ref, ref, self.cross[0].at[k], self.cross[1].at[k], h.xo).wait_recv()
            copy = remote(ref, ref, self.cross[2].at[k], self.cross[3].at[k], h.core)
            copy.start()
            self.sent.append(copy)
            yield

    def dz(self, k):
        return self.OFFSET[k] if not self.flip else (8 - self.OFFSET[k]) % 8

    def wait(self, way, r, k):
        h = self.here
        ref = self.region((h.z + self.dz(k)) % 8, h.c)
        m = way * 4 + r
        remote(ref, ref, self.send_sem.at[m], self.recv_sem.at[m], h.zp).wait_recv()

    def steps(self):
        first, second = (1, 0) if self.flip else (0, 1)
        self.push(first, 0)
        self.push(second, 0)
        self.share(0)
        yield
        for r in range(3):
            self.wait(first, r, 1 + 2 * r)
            self.push(first, r + 1)
            self.share(1 + 2 * r)
            self.wait(second, r, 2 + 2 * r)
            if r < 2:
                self.push(second, r + 1)
            self.share(2 + 2 * r)
            yield
        self.wait(first, 3, 7)
        self.share(7)
        yield

    def collect(self):
        h = self.here
        for k in range(8):
            ref = self.region((h.z + self.dz(k)) % 8, 1 - h.c)
            remote(ref, ref, self.core_send.at[k], self.core_recv.at[k], h.core).wait_recv()
            if self.cross:
                ref = self.region((h.z + self.dz(k)) % 8, 1 - h.c, 1 - h.xh)
                remote(ref, ref, self.cross[2].at[k], self.cross[3].at[k], h.core).wait_recv()

    def finish(self):
        for copy in self.sent:
            copy.wait_send()


def advance(steps, n=1):
    for _ in range(n):
        next(steps, None)


def kernel(
    hidden, gain_in, trace, counts, offsets, w_skv, w_eq, w_eo, w_cq, w_ckv, w_co, out,
    gain, hid, wproj, acc, ssq, kv_s, q_s, tr, picked, rows, enc_w, wck, woc, kvx, qx, qh, eq, ea, enc,
    att_own, attg, tail, attb,
    local, h_send, h_recv, k_send, k_recv, a_send, a_recv, kc_send, kc_recv,
    x_send, x_recv, r_ss, r_rs, r_cs, r_cr, s_xs, s_xr, s_cs, s_cr,
    p_send, p_recv, halo_send, halo_recv, tail_send, tail_recv,
):
    h = Here()
    c, t, s, z, xh, p = h.c, h.t, h.s, h.z, h.xh, h.p
    is_last = t == TP - 1

    barrier = pltpu.get_barrier_semaphore()
    greet = [h.at_tp(h.tp_peer(i)) for i in range(1, TP)]
    greet += [h.any_copy(dy, 1) for dy in range(4)]
    greet += [h.zp, h.zm, h.x2, h.core, h.last_before()]
    for device in greet:
        pl.semaphore_signal(barrier, inc=1, device_id=device, device_id_type=MESH)

    @pl.when(is_last)
    def _():
        for other in range(TP):
            pl.semaphore_signal(barrier, inc=1, device_id=h.at_after(other), device_id_type=MESH)

    pl.semaphore_wait(barrier, len(greet) + TP * (t // (TP - 1)))

    pushes = []

    def push(src, dst, send, recv, to):
        copy = remote(src, dst, send, recv, to)
        copy.start()
        pushes.append(copy)

    def came(ref, recv):
        remote(ref, ref, p_send.at[0, 0], recv, h.core).wait_recv()

    def bring(src, dst, i):
        copy = pltpu.make_async_copy(src, dst, local.at[i])
        copy.start()
        return copy

    def project(slot, part, index):
        here = pl.ds(part * 256, 256)
        wide = hid[slot, here, :].astype(F32)
        squares = jnp.sum(wide * wide, axis=-1, keepdims=True)
        scaled = (wide * gain[slot]).astype(BF)
        w = wproj[pl.ds(pl.multiple_of(slot * 512, 512), 512), :]
        product = dot(scaled, w)
        if index is None:
            ssq[here, :] = squares
            acc[here, :] = product
        else:
            ssq[here, :] += squares
            acc[here, :] += product

    def hid_gather(i):
        def region(slot, part, half):
            base = part * 256 + i * 128
            if half is None:
                return hid.at[slot, pl.ds(base, 128)]
            return hid.at[slot, pl.ds(base + half * 64, 64)]

        def own(part):
            return hidden.at[pl.ds(part * 256 + i * 128, 128)]

        def arrived(slot, part, index):
            if i == 1:
                project(slot, part, index)

        return Gather(h, region, own, h_send.at[i], h_recv.at[i], arrived, h.xp)

    gather_h = [hid_gather(0), hid_gather(1)]
    for g in gather_h:
        g.begin(0)
        g.begin(1)
    steps_h = [g.steps() for g in gather_h]

    mine = pl.ds(p * 8, 8)
    halves = pl.ds(c * 32, 32)
    push(trace, tr.at[mine], x_send.at[0], x_recv.at[0], h.x2)
    own_trace = bring(trace, tr.at[mine], 0)
    own_hid = bring(hidden, hid.at[t], 1)
    own_skv = bring(w_skv, wproj.at[:, pl.ds(0, 256)], 2)
    own_cq = bring(w_cq, wproj.at[:, pl.ds(256, 256)], 3)
    own_eq = bring(w_eq.at[halves], enc_w.at[0, s, c], 4)
    own_eo = bring(w_eo.at[halves], enc_w.at[1, s, c], 5)
    own_ckv = [bring(w_ckv.at[pl.ds(512 * i, 256)], wck.at[t, pl.ds(512 * i, 256)], 6 + i) for i in range(2)]
    ck_rows = pl.ds(c * 512 + 256 + z * 32, 32)
    own_ckv.append(bring(w_ckv.at[ck_rows], wck.at[t, ck_rows], 8))
    co_rows = pl.ds(z * 32 + c * 16, 16)
    own_co = bring(w_co.at[co_rows, pl.ds(pl.multiple_of(t * 512, 512), 512)], woc.at[t, z * 2 + c], 9)

    def ring(i, region, flip):
        return Ring(h, region, (r_ss.at[i], r_rs.at[i], r_cs.at[i], r_cr.at[i]), flip)

    def trace_ring(i, sel):
        return ring(i, lambda zz, cc: tr.at[pl.ds((cc * 16 + zz * 2 + sel) * 8, 8)], bool(i % 2))

    def enc_ring(i):
        w = i % 2
        return Ring(
            h, lambda zz, cc, sel=xh: enc_w.at[w, zz * 2 + sel, cc],
            (r_ss.at[i], r_rs.at[i], r_cs.at[i], r_cr.at[i]), bool(w),
            (s_xs.at[w], s_xr.at[w], s_cs.at[w], s_cr.at[w]),
        )

    def ckv_ring(i):
        return ring(
            i, lambda zz, cc: wck.at[pl.ds(4 * (i % 2), 4), pl.ds(cc * 512 + 256 + zz * 32, 32)], bool(i % 2)
        )

    def co_ring(i):
        return ring(i, lambda zz, cc: woc.at[pl.ds(4 * (i % 2), 4), zz * 2 + cc], bool(i % 2))

    rings_t = [trace_ring(0, xh), trace_ring(1, 1 - xh)]
    rings_e = [enc_ring(2), enc_ring(3)]
    rings_k = [ckv_ring(4), ckv_ring(5)]
    rings_o = [co_ring(6), co_ring(7)]
    rings = rings_t + rings_e + rings_k + rings_o
    steps_t, steps_e, steps_k2, steps_o = (
        [r.steps() for r in group] for group in (rings_t, rings_e, rings_k, rings_o)
    )

    own_trace.wait()
    advance(steps_t[0])
    came(tr.at[pl.ds((p + 1 - 2 * xh) * 8, 8)], x_recv.at[0])
    advance(steps_t[1])

    def wck_region(slot, part, half):
        base = c * 512 + part * 128
        if half is None:
            return wck.at[slot, pl.ds(base, 128)]
        return wck.at[slot, pl.ds(base + half * 64, 64)]

    def share(slot, part, index):
        ref = wck_region(slot, part, None)
        push(ref, ref, kc_send.at[index], kc_recv.at[index], h.core)

    gather_k = Gather(
        h, wck_region, lambda part: w_ckv.at[pl.ds(c * 512 + part * 128, 128)], k_send, k_recv, share, h.xo
    )
    gather_k.begin_x(0)
    gather_k.begin_x(1)
    steps_k = gather_k.steps()

    others = [(0, 1), (1, 0), (3, 0), (1, 1), (3, 1), (2, 0), (2, 1)]
    for i, (dy, other) in enumerate(others):
        push(w_ckv.at[ck_rows], wck.at[t, ck_rows], p_send.at[0, i], p_recv.at[0, i], h.any_copy(dy, other))
    for i, (dy, other) in enumerate(others):
        cols = pl.ds(pl.multiple_of(h.slot(dy, other) * 512, 512), 512)
        push(
            w_co.at[co_rows, cols], woc.at[t, z * 2 + c], p_send.at[1, i], p_recv.at[1, i],
            h.any_copy(dy, other),
        )

    for i in range(TP):
        gain[i] = gain_in[512 * i : 512 * (i + 1)].astype(F32).reshape(1, 512)
    own_hid.wait()
    own_skv.wait()
    own_cq.wait()
    project(t, 0, None)
    project(t, 1, None)

    def both(steps, n=1):
        for _ in range(n):
            for one in steps:
                advance(one)

    both(steps_h, 2)
    both(steps_t)
    both(steps_h, 3)
    both(steps_t)
    own_eq.wait()
    own_eo.wait()
    both(steps_e)
    both(steps_h, 3)
    both(steps_t)
    both(steps_e)
    both(steps_h, 2)
    both(steps_t)

    for r in rings_t:
        r.collect()

    def pick(owner):
        for k in range(4):
            at = p * 8 + owner - offsets[k, owner]
            at = jnp.minimum(jnp.maximum(at, 0), 254)
            picked[owner, 128 * k : 128 * k + 64, :] = tr[at]
            picked[owner, 128 * k + 64 : 128 * k + 128, :] = tr[at + 1]

    columns = pl.ds(pl.multiple_of(t * 128, 128), 128)
    for i in range(1, TP):
        to = h.tp_peer(i)
        pick(to)
        push(picked.at[to], rows.at[:, columns], p_send.at[3, i], p_recv.at[3, i], h.at_tp(to))
    pick(t)
    rows[:, columns] = picked[t]

    both(steps_h, 2)
    both(steps_e)
    for copy in own_ckv:
        copy.wait()
    for i, (dy, other) in enumerate(others):
        came(wck.at[h.slot(4 - dy, other), ck_rows], p_recv.at[0, i])
    both(steps_k2)
    both(steps_h, 2)

    inverse = lax.rsqrt(ssq[...] * (1.0 / 4096) + EPS)
    projected = (acc[...] * inverse).astype(BF)
    kv_s[...] = projected[:, :256]
    q_s[0:512, :] = projected[:, 256:]
    q_s[512:576, :] = jnp.zeros((64, 256), BF)
    for i in range(1, TP):
        to = h.tp_peer(i)
        mine_there = pl.ds(pl.multiple_of(to * 64, 64), 64)
        push(kv_s.at[mine_there], kvx.at[t], p_send.at[2, i], p_recv.at[2, i], h.at_tp(to))
    kvx[t] = kv_s[pl.ds(pl.multiple_of(t * 64, 64), 64), :]

    for i in range(1, TP):
        to = h.tp_peer(i)
        mine_there = pl.ds(pl.multiple_of(to * 64 + 48, 16), 80)
        push(q_s.at[mine_there], qx.at[t], p_send.at[4, i], p_recv.at[4, i], h.at_tp(to))
    qx[t] = q_s[pl.ds(pl.multiple_of(t * 64 + 48, 16), 80), :]
    push(q_s.at[pl.ds(0, 64)], qh.at[t], halo_send.at[0], halo_recv.at[t], h.last_before())

    gather_k.begin_y(1)
    gather_k.begin_y(0)
    both(steps_e)
    swaps = [r.swap() for r in rings_e]
    both(swaps, 3)
    both(steps_e)
    both(swaps, 2)
    both(steps_k2)
    own_co.wait()
    for i, (dy, other) in enumerate(others):
        came(woc.at[h.slot(4 - dy, other), z * 2 + c], p_recv.at[1, i])

    def from_peer(i):
        return h.tp_peer(TP - i)

    for i in range(1, TP):
        cols = pl.ds(pl.multiple_of(from_peer(i) * 128, 128), 128)
        came(rows.at[:, cols], p_recv.at[3, i])
    advance(steps_k, 1)
    both(swaps, 3)
    both(steps_k2)
    for r in rings_e:
        r.collect()
    for n in range(4):
        cols = slice(256 * n, 256 * (n + 1))
        eq[:, cols] = dot(rows[...], enc_w[0, :, :, :, cols].reshape(1024, 256)).astype(BF)
    advance(steps_k, 2)
    both(steps_k2)
    for i in range(1, TP):
        came(kvx.at[from_peer(i)], p_recv.at[2, i])
    advance(steps_k, 2)
    for e in range(8):
        cols = slice(128 * e, 128 * (e + 1))
        scores = dot_t(eq[:, cols], kvx[e, :, :128]) * FACTOR
        top = jnp.max(scores, axis=-1, keepdims=True)
        weights = jnp.exp(scores - top)
        probs = (weights * (1.0 / jnp.sum(weights, axis=-1, keepdims=True))).astype(BF)
        ea[:, cols] = dot(probs, kvx[e, :, 128:]).astype(BF)
        advance(steps_k, 1)
        if e == 3:
            both(steps_k2)
            both(steps_o)
    for n in range(4):
        cols = slice(256 * n, 256 * (n + 1))
        update = dot(ea[...], enc_w[1, :, :, :, cols].reshape(1024, 256))
        enc[:, cols] = (rows[:, cols].astype(F32) + update).astype(BF)
        advance(steps_k, 1)
    both(steps_k2)
    both(steps_o)

    for i in range(1, TP):
        came(qx.at[from_peer(i)], p_recv.at[4, i])

    @pl.when(is_last)
    def _():
        for j in range(TP):
            came(qh.at[j], halo_recv.at[j])
            qx[j, 16:80, :] = qh[j]

    for index, (slot, part) in enumerate(gather_k.order()):
        came(wck.at[slot, pl.ds((1 - c) * 512 + part * 128, 128)], kc_recv.at[index])
    for r in rings_k:
        r.collect()

    live_keys = counts[t] * 128
    mask = lax.broadcasted_iota(jnp.int32, (160, 512), 1) < live_keys
    any_live = jnp.zeros((64, 128), jnp.int32) + live_keys > 0
    last_row = lax.broadcasted_iota(jnp.int32, (64, 128), 0) == 63

    def att_gather(i):
        def region(slot, part, half):
            base = i * 1024 + part * 512
            if half is None:
                return attg.at[slot, :, pl.ds(base, 512)]
            return attg.at[slot, :, pl.ds(base + half * 256, 256)]

        def own(part):
            return att_own.at[:, pl.ds(i * 1024 + part * 512, 512)]

        return Gather(h, region, own, a_send.at[i], a_recv.at[i], lambda *_: None, h.xp)

    gather_a = [att_gather(0), att_gather(1)]
    steps_a = [g.steps() for g in gather_a]

    def tail_copy(j):
        return remote(
            att_own.at[:, pl.ds(256 * j, 256)], tail.at[j],
            tail_send.at[j], tail_recv.at[0], h.at_after(j),
        )

    for j in range(TP):
        pair = dot(enc[...], wck[j]).astype(BF)
        scores = jnp.concatenate(
            [dot_t(qx[j, :, 128 * i : 128 * i + 128], pair[:, 256 * i : 256 * i + 128]) for i in range(2)], axis=0
        )
        scores = jnp.where(mask, scores * FACTOR, NEG)
        weights = jnp.exp(scores - jnp.max(scores, axis=-1, keepdims=True))
        probs = (weights * (1.0 / jnp.sum(weights, axis=-1, keepdims=True))).astype(BF)
        for i in range(2):
            mixed = dot(probs[80 * i : 80 * i + 80], pair[:, 256 * i + 128 : 256 * i + 256])
            mixed = jnp.where(last_row, mixed[15:16], mixed[16:80])
            at = 256 * j + 128 * i
            att_own[:, at : at + 128] = jnp.where(any_live, mixed, 0.0).astype(BF)

        @pl.when(is_last)
        def _():
            tail_copy(j).start()

        if j == 1:
            gather_a[0].begin(0)
        if j == 3:
            gather_a[0].begin(1)
            both(steps_o)
        if j == 3:
            advance(steps_a[0], 1)
        if j == 5:
            advance(steps_a[0], 2)
        if j == 5:
            gather_a[1].begin(0)
            both(steps_o)
        if j == 6:
            advance(steps_a[0], 2)
        if j == 7:
            advance(steps_a[0], 1)
    gather_a[1].begin(1)
    advance(steps_a[1], 1)
    advance(steps_a[0], 1)
    both(steps_o)
    advance(steps_a[0], 1)
    advance(steps_a[1], 2)
    came(tail.at[t], tail_recv.at[0])
    for i in range(1, TP):
        push(tail.at[t], tail.at[t], p_send.at[5, i], p_recv.at[5, i], h.at_tp(h.tp_peer(i)))
    advance(steps_a[0], 2)
    advance(steps_a[1], 2)
    advance(steps_a[0], 3)
    advance(steps_a[1], 3)
    advance(steps_a[0], 2)
    attg[t] = att_own[...]
    for i in range(1, TP):
        came(tail.at[from_peer(i)], p_recv.at[5, i])
    for r in rings_o:
        r.collect()

    own_row = lax.broadcasted_iota(jnp.int32, (16, 1024), 0) == 15

    def attended(i):
        cols = slice(1024 * i, 1024 * (i + 1))
        for j in range(4 * i, 4 * i + 4):
            attb[0:64, 256 * j : 256 * (j + 1)] = jnp.where(p > 0, tail[j].astype(F32), 0.0).astype(BF)
        for v in range(TP):
            if v:
                attb[64 * v : 64 * v + 64, cols] = attg[v - 1, :, cols]
            attb[64 * v + 48 : 64 * v + 64, cols] = jnp.where(
                own_row, attg[v, 48:64, cols], attb[64 * v + 48 : 64 * v + 64, cols]
            )
        return dot(attb[:, cols], woc[4 * i : 4 * i + 4].reshape(1024, 512))

    acc[...] = hid[t].astype(F32) + attended(0)
    advance(steps_a[1], 7)
    out[...] = (acc[...] + attended(1)).astype(BF)

    for group in gather_h + [gather_k] + gather_a + rings:
        group.finish()
    for copy in pushes:
        copy.wait_send()

    @pl.when(is_last)
    def _():
        for j in range(TP):
            tail_copy(j).wait_send()


def body(hidden, gain, trace, counts, offsets, w_skv, w_eq, w_eo, w_cq, w_ckv, w_co):
    any_ = pl.BlockSpec(memory_space=pl.ANY)
    vmem = pl.BlockSpec(memory_space=pltpu.VMEM)
    smem = pl.BlockSpec(memory_space=pltpu.SMEM)
    dma = pltpu.SemaphoreType.DMA
    v = pltpu.VMEM
    scratch = [
        v((8, 1, 512), F32),
        v((8, 512, 512), BF),
        v((4096, 512), BF),
        v((512, 512), F32),
        v((512, 1), F32),
        v((512, 256), BF),
        v((576, 256), BF),
        v((256, 64, 128), BF),
        v((8, 512, 128), BF),
        v((512, 1024), BF),
        v((2, 16, 2, 32, 1024), BF),
        v((8, 1024, 512), BF),
        v((8, 16, 16, 512), BF),
        v((8, 64, 256), BF),
        v((8, 80, 256), BF),
        v((8, 64, 256), BF),
        v((512, 1024), BF),
        v((512, 1024), BF),
        v((512, 1024), BF),
        v((64, 2048), BF),
        v((8, 64, 2048), BF),
        v((8, 64, 256), BF),
        v((512, 2048), BF),
        dma((10,)),
        dma((2, 18)), dma((2, 18)), dma((18,)), dma((18,)), dma((2, 18)), dma((2, 18)), dma((14,)), dma((14,)),
        dma((3,)), dma((3,)),
        dma((8, 8)), dma((8, 8)), dma((8, 8)), dma((8, 8)),
        dma((2, 8)), dma((2, 8)), dma((2, 8)), dma((2, 8)),
        dma((6, 8)), dma((6, 8)),
        dma((1,)), dma((8,)), dma((8,)), dma((1,)),
    ]
    return pl.pallas_call(
        kernel,
        out_shape=jax.ShapeDtypeStruct((512, 512), BF),
        in_specs=[any_, vmem, any_, smem, smem, any_, any_, any_, any_, any_, any_],
        out_specs=vmem,
        scratch_shapes=scratch,
        compiler_params=pltpu.CompilerParams(
            collective_id=0, has_side_effects=True, vmem_limit_bytes=58 << 20
        ),
        cost_estimate=pl.CostEstimate(flops=11_000_000_000, bytes_accessed=14_000_000, transcendentals=1_000_000),
    )(
        hidden, gain, trace.reshape(8, 64, 128), counts, offsets.T,
        w_skv, w_eq, w_eo, w_cq, w_ckv, w_co,
    )


def solution(mesh):
    place = ("seq", "section")
    in_specs = (
        P(place, "tp"), P(), P(place, "tp"), P(place), P(place, None), P(None, "tp"),
        P("section", None), P("section", None), P(None, "tp"), P(None, "tp"), P("tp", None),
    )
    return jax.shard_map(body, mesh=mesh, in_specs=in_specs, out_specs=P(place, "tp"), check_vma=False)
```
